32 devices in a mesh: ctx: 8 (over z, y), seq: 4 (over x, core).
Axes of the slice: x: 2, y: 2, z: 4, core: 2. Of those that a mesh axis runs over, the one named last changes fastest.
Arguments:
- query_input: bfloat16 [4, 1024, 2048], P('seq', 'ctx'), may hold values from -6 to 6
- key_input: bfloat16 [4, 1024, 2048], P('seq', 'ctx'), may hold values from -6 to 6
- value_input: bfloat16 [4, 1024, 2048], P('seq', 'ctx'), may hold values from -6 to 6
- cotangent: bfloat16 [4, 1024, 2048], P('seq', 'ctx'), may hold values from -6 to 6
- residues: float32 [2048, 16], replicated, may hold values from -1.5 to 1.5
- decay_rates: float32 [2048, 16], replicated, as said below
Outputs:
- output: bfloat16 [4, 1024, 2048], P('seq', 'ctx')
- grad_query: bfloat16 [4, 1024, 2048], P('seq', 'ctx')
- grad_key: bfloat16 [4, 1024, 2048], P('seq', 'ctx')
- grad_value: bfloat16 [4, 1024, 2048], P('seq', 'ctx')
- grad_residues: float32 [2048, 16], replicated
The draws below stay inside these ranges and needn't reach their ends.
Inputs may be any that keep to these rules, and one draw needn't show every extreme that they name: `decay_rates`: every rate lies between 0.1 divided by 1024 and 1 divided by 30.
All inputs are finite; a program needn't handle non-finite values.
Results may differ from the reference program's by a relative error of at most 0.0013.
Values sent between devices are 32-bit elements; how exact they have to be, the bound alone decides.
A program may use at most 192 MiB of HBM per device.

```python
import jax
import jax.numpy as jnp
from jax import lax

C = 2048
M = 16
TOK_DEV = 128
SEQ_LEN = 1024
BATCH = 4


def draw_decay_rates(key, part):
    key = jax.random.fold_in(key, 7)
    pick_key, slow_key, fast_key = jax.random.split(key, 3)
    share = 0.5
    slow = jax.random.uniform(pick_key, (C, M)) < share
    slow_rate = jnp.exp(jax.random.uniform(slow_key, (C, M), minval=jnp.log(0.05), maxval=0.0)) * (2.0 / SEQ_LEN)
    fast_rate = jnp.exp(jax.random.uniform(fast_key, (C, M), minval=jnp.log(1.0 / (4 * TOK_DEV)), maxval=jnp.log(1.0 / 30)))
    return jnp.where(slow, slow_rate, fast_rate).astype(jnp.float32)


def levels(own_key, dims, shards, least, high):
    loudness, own = 1.0, jax.random.fold_in(own_key, 6)
    for dim, shards_of in shards:
        heights = jnp.exp(jax.random.uniform(jax.random.fold_in(own, dim), (shards_of,), jnp.float32, least / len(shards), high / len(shards)))
        loudness = loudness * jnp.repeat(heights, dims[dim] // shards_of).reshape([-1 if axis == dim else 1 for axis in range(len(dims))])
    return loudness


def gaussian(stream_key, dims, scale, most, cuts=(), dtype=jnp.bfloat16):
    result = scale * jax.random.normal(stream_key, dims, jnp.float32)
    if cuts:
        result = result * levels(stream_key, dims, cuts, -0.22, 0.18)
    return jnp.clip(result, -most, most).astype(dtype)


def setup_inputs(seed: int = 0) -> dict:
    arg_keys = jax.random.split(jax.random.key(seed), 7)
    query_input = gaussian(arg_keys[0], (BATCH, SEQ_LEN, C), 1.0, 6.0, ((0, 4), (1, 8)))
    key_input = gaussian(arg_keys[1], (BATCH, SEQ_LEN, C), 1.0, 6.0, ((0, 4), (1, 8)))
    value_input = gaussian(arg_keys[2], (BATCH, SEQ_LEN, C), 1.0, 6.0, ((0, 4), (1, 8)))
    cotangent = gaussian(arg_keys[3], (BATCH, SEQ_LEN, C), 1.0, 6.0, ((0, 4), (1, 8)))
    residues = gaussian(arg_keys[4], (C, M), 0.25, 1.5, (), jnp.float32)
    decay_rates = draw_decay_rates(jax.random.fold_in(arg_keys[6], 71), 0)
    return dict(query_input=query_input, key_input=key_input, value_input=value_input, cotangent=cotangent, residues=residues, decay_rates=decay_rates)


def filter_taps(residues, decay_rates, scaling, steps):
    taps = jnp.zeros((SEQ_LEN, C), jnp.float32)
    for mode_index in range(M):
        weight = residues[:, mode_index] * scaling[:, mode_index]
        taps = taps + weight[None, :] * jnp.exp(-steps[:, None] * decay_rates[None, :, mode_index])
    return taps

def reference(query_input, key_input, value_input, cotangent, residues, decay_rates):
    scaling = jnp.sqrt(-jnp.expm1(-2.0 * decay_rates))
    steps = jnp.arange(SEQ_LEN).astype(jnp.float32)
    taps = filter_taps(residues, decay_rates, scaling, steps)
    padded = 2 * SEQ_LEN
    tap_spec = jnp.fft.rfft(taps, n=padded, axis=0)

    def per_sequence(carried, sequence_parts):
        query_rows, key_rows, value_rows, cot_rows = sequence_parts
        query_wide = query_rows.astype(jnp.float32)
        key_wide = key_rows.astype(jnp.float32)
        value_wide = value_rows.astype(jnp.float32)
        cot_wide = cot_rows.astype(jnp.float32)
        mixed = key_wide * value_wide
        adjoint = cot_wide * query_wide
        mix_spec = jnp.fft.rfft(mixed, n=padded, axis=0)
        adj_spec = jnp.fft.rfft(adjoint, n=padded, axis=0)
        convolved = jnp.fft.irfft(mix_spec * tap_spec, n=padded, axis=0)[:SEQ_LEN]
        grad_mixed = jnp.fft.irfft(adj_spec * jnp.conj(tap_spec), n=padded, axis=0)[:SEQ_LEN]
        lagged = jnp.fft.irfft(adj_spec * jnp.conj(mix_spec), n=padded, axis=0)[:SEQ_LEN]
        results = ((query_wide * convolved).astype(jnp.bfloat16), (cot_wide * convolved).astype(jnp.bfloat16), (grad_mixed * value_wide).astype(jnp.bfloat16), (grad_mixed * key_wide).astype(jnp.bfloat16))
        return (carried + lagged, results)
    lagged, stacked = lax.scan(per_sequence, jnp.zeros((SEQ_LEN, C), jnp.float32), (query_input, key_input, value_input, cotangent))
    output, grad_query, grad_key, grad_value = stacked
    columns = []
    for mode_index in range(M):
        decay = jnp.exp(-steps[:, None] * decay_rates[None, :, mode_index])
        columns.append(lax.optimization_barrier(jnp.sum(lagged * decay, axis=0)))
    grad_residues = jnp.stack(columns, axis=1) * scaling / (BATCH * SEQ_LEN)
    return (output, grad_query, grad_key, grad_value, grad_residues)
```

```python
import functools

import jax
import jax.numpy as jnp
from jax import lax
from jax.experimental import pallas as pl
from jax.experimental.pallas import tpu as pltpu
from jax.sharding import PartitionSpec as P

SUB = 8
LANES = 128
MESH = pl.DeviceIdType.MESH
F32 = jnp.float32


def one_minus_exp(u):
    total = jnp.ones_like(u)
    for order in range(8, 1, -1):
        total = 1.0 - (u / order) * total
    return u * total


def columns_of(block):
    return pl.ds(pl.multiple_of(block * LANES, LANES), LANES)


def kernel(
    n_ctx, n_seq, query, key, value, cot, res_ref, rate_ref,
    out, grad_query, grad_key, grad_value, grad_res,
    query_p, key_p, value_p, cot_p, mix_p, adj_p, conv_p, back_p, before, after,
    lam_row, lam16_row, weight_row, rate_tile, scale_tile,
    state_out, state_in, carry_out, carry_in, lag_out, lag_in, part_in, grad_all,
    state_send, state_recv, carry_send, carry_recv, lag_send, lag_recv,
    part_send, part_recv, grad_send, grad_recv,
):
    me = lax.axis_index("ctx")
    my_seq = lax.axis_index("seq")
    length, channels = query.shape
    modes = res_ref.shape[0]
    steps = length // SUB
    n_blocks = channels // LANES
    halves = modes // SUB
    n_tiles = n_blocks * halves
    per_owner = n_tiles // n_ctx
    owners_per_group = max(1, halves // per_owner)
    blocks_per_group = max(1, per_owner // halves)
    n_groups = n_ctx // owners_per_group
    my_group = me // owners_per_group

    def peer(distance):
        return lax.rem(me + distance, n_ctx)

    def seq_peer(distance):
        return lax.rem(my_seq + distance, n_seq)

    def remote(src, dst, send, recv, target):
        return pltpu.make_async_remote_copy(
            src_ref=src, dst_ref=dst, send_sem=send, recv_sem=recv,
            device_id=target, device_id_type=MESH,
        )

    def owned(ref, owner):
        return ref.at[pl.ds(owner * per_owner, per_owner)]

    def state_copy(owner, slot):
        return remote(owned(state_out, owner), state_in.at[slot], state_send.at[owner], state_recv.at[slot], {"ctx": owner})

    def lag_copy(owner, slot):
        return remote(owned(lag_out, owner), lag_in.at[slot], lag_send.at[owner], lag_recv.at[slot], {"ctx": owner})

    def carry_copy(target, slot):
        return remote(carry_out.at[target], owned(carry_in, slot), carry_send.at[target], carry_recv.at[slot], {"ctx": target})

    def part_copy(target, slot):
        return remote(part_in.at[my_seq], part_in.at[slot], part_send.at[target], part_recv.at[slot], {"seq": target})

    def grad_copy(target, slot):
        return remote(owned(grad_all, me), owned(grad_all, slot), grad_send.at[target], grad_recv.at[slot], {"ctx": target})

    barrier = pltpu.get_barrier_semaphore()
    for distance in range(1, n_ctx):
        pl.semaphore_signal(barrier, inc=1, device_id={"ctx": peer(distance)}, device_id_type=MESH)
    for distance in range(1, n_seq):
        pl.semaphore_signal(barrier, inc=1, device_id={"seq": seq_peer(distance)}, device_id_type=MESH)

    for block in range(n_blocks):
        cols = slice(block * LANES, (block + 1) * LANES)
        rate = rate_ref[:, cols]
        scale = jnp.sqrt(one_minus_exp(2.0 * rate))
        lam_row[block] = jnp.exp(-rate)
        lam16_row[block] = jnp.exp(-float(steps) * rate)
        weight_row[block] = res_ref[:, cols] * scale
        for half in range(halves):
            rows = slice(half * SUB, (half + 1) * SUB)
            rate_tile[block * halves + half] = rate[rows]
            scale_tile[block * halves + half] = scale[rows]

    row = lax.broadcasted_iota(jnp.int32, (length, length), 0)
    col = lax.broadcasted_iota(jnp.int32, (length, length), 1)
    to_steps = jnp.where(col == steps * (row % SUB) + row // SUB, 1.0, 0.0).astype(jnp.bfloat16)
    to_tokens = jnp.where(row == steps * (col % SUB) + col // SUB, 1.0, 0.0).astype(jnp.bfloat16)
    sub = lax.broadcasted_iota(jnp.int32, (SUB, LANES), 0)
    sub_f = sub.astype(F32)

    def wide(ref, block, mode):
        return jnp.broadcast_to(ref[block, pl.ds(mode, 1), :], (SUB, LANES))

    def cut(array):
        return [array[step * SUB:(step + 1) * SUB] for step in range(steps)]

    def states_of(block):
        cols = columns_of(block)

        def turned(ref):
            return jnp.dot(to_steps, ref[:, cols], preferred_element_type=F32)

        key_here, value_here, query_here, cot_here = turned(key), turned(value), turned(query), turned(cot)
        query_p[block], key_p[block], value_p[block], cot_p[block] = query_here, key_here, value_here, cot_here
        mixed = key_here * value_here
        adjoint = cot_here * query_here
        mix_p[block] = mixed
        adj_p[block] = adjoint
        mix, adj = cut(mixed), cut(adjoint)
        for mode in range(modes):
            tile, place = block * halves + mode // SUB, mode % SUB
            lam = wide(lam_row, block, mode)
            lam16 = wide(lam16_row, block, mode)
            last = mix[0]
            first = adj[-1]
            for step in range(1, steps):
                last = last * lam + mix[step]
                first = first * lam + adj[steps - 1 - step]
            up, down, power = last, first, lam16
            for shift in (1, 2, 4):
                up = up + jnp.where(sub >= shift, power, 0.0) * pltpu.roll(up, shift, 0)
                down = down + jnp.where(sub < SUB - shift, power, 0.0) * pltpu.roll(down, SUB - shift, 0)
                power = power * power
            ahead = jnp.where(sub >= 1, pltpu.roll(up, 1, 0), 0.0)
            before[block, mode] = ahead
            after[block, mode] = jnp.where(sub < SUB - 1, pltpu.roll(down, SUB - 1, 0), 0.0)
            state_out[tile, 0, pl.ds(place, 1), :] = up[SUB - 1:SUB]
            state_out[tile, 1, pl.ds(place, 1), :] = down[0:1]
            lag_out[tile, pl.ds(place, 1), :] = jnp.sum(first * ahead, axis=0, keepdims=True)

    def first_pass(index, _):
        group = lax.rem(my_group + index, n_groups)

        def one(inner, _):
            states_of(group * blocks_per_group + inner)
            return 0

        lax.fori_loop(0, blocks_per_group, one, 0)

        @pl.when(index == 1)
        def _():
            pl.semaphore_wait(barrier, n_ctx - 1 + n_seq - 1)

        for inner in range(owners_per_group):
            owner = group * owners_per_group + inner

            @pl.when(owner != me)
            def _():
                state_copy(owner, me).start()

            @pl.when(owner == me)
            def _():
                state_in[me] = state_out[pl.ds(me * per_owner, per_owner)]

        return 0

    lax.fori_loop(1, n_groups + 1, first_pass, 0)

    def chunk_terms(block):
        mix = cut(mix_p[block])
        adj = cut(adj_p[block])
        lam = [lam_row[block, pl.ds(half * SUB, SUB), :] for half in range(halves)]
        power = [weight_row[block, pl.ds(half * SUB, SUB), :] for half in range(halves)]
        taps = []
        for step in range(steps):
            taps.append(jnp.broadcast_to(jnp.sum(sum(power), axis=0, keepdims=True), (SUB, LANES)))
            power = [left * right for left, right in zip(power, lam)]
        for step in range(steps):
            total = taps[0] * mix[step]
            for other in range(step):
                total = total + taps[step - other] * mix[other]
            conv_p[block, pl.ds(step * SUB, SUB), :] = total
            total = taps[0] * adj[step]
            for other in range(step + 1, steps):
                total = total + taps[other - step] * adj[other]
            back_p[block, pl.ds(step * SUB, SUB), :] = total
        sums = [None] * halves
        for lag in range(steps - 1, -1, -1):
            total = adj[lag] * mix[0]
            for step in range(lag + 1, steps):
                total = total + adj[step] * mix[step - lag]
            level = jnp.broadcast_to(jnp.sum(total, axis=0, keepdims=True), (SUB, LANES))
            sums = [level if have is None else have * left + level for have, left in zip(sums, lam)]
        for half in range(halves):
            tile = block * halves + half
            lag_out[tile] = sums[half] + lam[half] * lag_out[tile]

    def second_pass(index, _):
        group = lax.rem(my_group + index, n_groups)

        def one(inner, _):
            chunk_terms(group * blocks_per_group + inner)
            return 0

        lax.fori_loop(0, blocks_per_group, one, 0)
        for inner in range(owners_per_group):
            owner = group * owners_per_group + inner

            @pl.when(owner != me)
            def _():
                lag_copy(owner, me).start()

            @pl.when(owner == me)
            def _():
                lag_in[me] = lag_out[pl.ds(me * per_owner, per_owner)]

        return 0

    lax.fori_loop(1, n_groups + 1, second_pass, 0)

    for distance in range(1, n_ctx):
        source = peer(n_ctx - distance)
        state_copy(source, source).wait_recv()
    for place in range(per_owner):
        rate = rate_tile[me * per_owner + place]
        lam = jnp.exp(-rate)
        hop = jnp.exp(-float(length) * rate)
        carried = jnp.zeros((SUB, LANES), F32)
        cross = jnp.zeros((SUB, LANES), F32)
        for source in range(n_ctx):
            carry_out[source, place, 0] = carried
            cross = cross + carried * state_in[source, place, 1]
            carried = carried * hop + state_in[source, place, 0]
        part_in[my_seq, place] = lam * cross
        carried = jnp.zeros((SUB, LANES), F32)
        for source in range(n_ctx - 1, -1, -1):
            carry_out[source, place, 1] = carried
            carried = carried * hop + state_in[source, place, 1]
    for distance in range(1, n_ctx):
        carry_copy(peer(distance), me).start()
    carry_in[pl.ds(me * per_owner, per_owner)] = carry_out[me]

    for distance in range(1, n_ctx):
        source = peer(n_ctx - distance)
        lag_copy(source, source).wait_recv()
    for place in range(per_owner):
        total = part_in[my_seq, place]
        for source in range(n_ctx):
            total = total + lag_in[source, place]
        part_in[my_seq, place] = total * scale_tile[me * per_owner + place]
    for distance in range(1, n_seq):
        part_copy(seq_peer(distance), my_seq).start()

    def finish(block):
        cols = columns_of(block)
        conv = cut(conv_p[block])
        back = cut(back_p[block])
        for mode in range(modes):
            tile, place = block * halves + mode // SUB, mode % SUB
            lam = wide(lam_row, block, mode)
            lead = lam * wide(weight_row, block, mode)
            rate = jnp.broadcast_to(rate_tile[tile, pl.ds(place, 1), :], (SUB, LANES)) * float(steps)
            carried = jnp.broadcast_to(carry_in[tile, 0, pl.ds(place, 1), :], (SUB, LANES))
            term = lead * (before[block, mode] + jnp.exp(-sub_f * rate) * carried)
            carried = jnp.broadcast_to(carry_in[tile, 1, pl.ds(place, 1), :], (SUB, LANES))
            other = lead * (after[block, mode] + jnp.exp((sub_f - (SUB - 1.0)) * rate) * carried)
            for step in range(steps):
                conv[step] = conv[step] + term
                back[steps - 1 - step] = back[steps - 1 - step] + other
                if step + 1 < steps:
                    term = term * lam
                    other = other * lam
        conv = jnp.concatenate(conv, axis=0)
        back = jnp.concatenate(back, axis=0)

        def put(ref, wide_result):
            rounded = wide_result.astype(jnp.bfloat16)
            ref[:, cols] = jnp.dot(to_tokens, rounded, preferred_element_type=F32).astype(jnp.bfloat16)

        put(out, query_p[block] * conv)
        put(grad_query, cot_p[block] * conv)
        put(grad_key, value_p[block] * back)
        put(grad_value, key_p[block] * back)

    def last_pass(index, _):
        group = lax.rem(my_group + n_groups - index, n_groups)
        for inner in range(owners_per_group):
            owner = group * owners_per_group + inner

            @pl.when(owner != me)
            def _():
                carry_copy(owner, owner).wait_recv()

        def one(inner, _):
            finish(group * blocks_per_group + inner)
            return 0

        lax.fori_loop(0, blocks_per_group, one, 0)

        @pl.when(index == n_groups // 2)
        def _():
            for distance in range(1, n_seq):
                source = seq_peer(n_seq - distance)
                part_copy(source, source).wait_recv()
            for place in range(per_owner):
                total = part_in[0, place]
                for source in range(1, n_seq):
                    total = total + part_in[source, place]
                grad_all[me * per_owner + place] = total * (1.0 / (length * n_ctx * n_seq))
            for distance in range(1, n_ctx):
                grad_copy(peer(distance), me).start()

        return 0

    lax.fori_loop(0, n_groups, last_pass, 0)

    for distance in range(1, n_ctx):
        source = peer(n_ctx - distance)
        grad_copy(source, source).wait_recv()
    for block in range(n_blocks):
        for half in range(halves):
            grad_res[half * SUB:(half + 1) * SUB, block * LANES:(block + 1) * LANES] = grad_all[block * halves + half]

    for distance in range(1, n_ctx):
        target = peer(distance)
        state_copy(target, me).wait_send()
        lag_copy(target, me).wait_send()
        carry_copy(target, me).wait_send()
        grad_copy(target, me).wait_send()
    for distance in range(1, n_seq):
        part_copy(seq_peer(distance), my_seq).wait_send()


def on_device(n_ctx, n_seq, query_input, key_input, value_input, cotangent, residues, decay_rates):
    _, length, channels = query_input.shape
    modes = residues.shape[1]
    n_blocks = channels // LANES
    halves = modes // SUB
    n_tiles = n_blocks * halves
    per_owner = n_tiles // n_ctx

    def rows():
        return pltpu.VMEM((n_blocks, length, LANES), F32)

    def tiles(*leading):
        return pltpu.VMEM(leading + (SUB, LANES), F32)

    signal = jax.ShapeDtypeStruct((length, channels), jnp.bfloat16)
    vmem = pl.BlockSpec(memory_space=pltpu.VMEM)
    results = pl.pallas_call(
        functools.partial(kernel, n_ctx, n_seq),
        out_shape=[signal] * 4 + [jax.ShapeDtypeStruct((modes, channels), F32)],
        in_specs=[vmem] * 6,
        out_specs=[vmem] * 5,
        scratch_shapes=[rows() for _ in range(8)]
        + [tiles(n_blocks, modes), tiles(n_blocks, modes)]
        + [pltpu.VMEM((n_blocks, modes, LANES), F32) for _ in range(3)]
        + [tiles(n_tiles), tiles(n_tiles)]
        + [
            tiles(n_tiles, 2), tiles(n_ctx, per_owner, 2),
            tiles(n_ctx, per_owner, 2), tiles(n_tiles, 2),
            tiles(n_tiles), tiles(n_ctx, per_owner),
            tiles(n_seq, per_owner), tiles(n_tiles),
        ]
        + [pltpu.SemaphoreType.DMA((n_ctx,)) for _ in range(6)]
        + [pltpu.SemaphoreType.DMA((n_seq,)) for _ in range(2)]
        + [pltpu.SemaphoreType.DMA((n_ctx,)) for _ in range(2)],
        compiler_params=pltpu.CompilerParams(
            collective_id=0, has_side_effects=True, vmem_limit_bytes=48 * 1024 * 1024
        ),
        cost_estimate=pl.CostEstimate(flops=100_000_000, bytes_accessed=4_500_000, transcendentals=1_000_000),
        name="modal_states",
    )(query_input[0], key_input[0], value_input[0], cotangent[0], residues.T, decay_rates.T)
    return tuple(array[None] for array in results[:4]) + (results[4].T,)


def solution(mesh):
    wide = P("seq", "ctx", None)
    return jax.shard_map(
        functools.partial(on_device, mesh.shape["ctx"], mesh.shape["seq"]),
        mesh=mesh,
        in_specs=(wide, wide, wide, wide, P(), P()),
        out_specs=(wide, wide, wide, wide, P()),
        check_vma=False,
    )
```

```python
import functools

import jax
import jax.numpy as jnp
from jax import lax
from jax.experimental import pallas as pl
from jax.experimental.pallas import tpu as pltpu
from jax.sharding import PartitionSpec as P

SUB = 8
LANES = 128
MESH = pl.DeviceIdType.MESH
F32 = jnp.float32


def one_minus_exp(u):
    total = jnp.ones_like(u)
    for order in range(8, 1, -1):
        total = 1.0 - (u / order) * total
    return u * total


def columns_of(block):
    return pl.ds(pl.multiple_of(block * LANES, LANES), LANES)


def step_order(length, steps, inverse):
    row = lax.broadcasted_iota(jnp.int32, (length, length), 0)
    col = lax.broadcasted_iota(jnp.int32, (length, length), 1)
    if inverse:
        row, col = col, row
    return jnp.where(col == steps * (row % SUB) + row // SUB, 1.0, 0.0).astype(jnp.bfloat16)


def kernel(
    n_ctx, n_seq, n_parts, query_hbm, key_hbm, value_hbm, cot_hbm, res_hbm, rate_hbm,
    out, grad_query, grad_key, grad_value, grad_res,
    query, key, value, cot, res_ref, rate_ref,
    query_p, key_p, value_p, cot_p, mix_p, adj_p, conv_p, back_p, before, after, up_turn, down_turn,
    lam_row, lam16_row, weight_row, rate_tile, scale_tile,
    state_out, state_in, carry_out, carry_in, lag_out, lag_in, part_in, grad_all,
    state_send, state_recv, carry_send, carry_recv, lag_send, lag_recv,
    part_send, part_recv, grad_send, grad_recv, load_sem, param_sem,
):
    me = lax.axis_index("ctx")
    my_seq = lax.axis_index("seq")
    length, channels = query.shape
    modes = res_ref.shape[0]
    steps = length // SUB
    n_blocks = channels // LANES
    halves = modes // SUB
    n_tiles = n_blocks * halves
    per_owner = n_tiles // n_ctx
    owners_per_group = max(1, halves // per_owner)
    blocks_per_group = max(1, per_owner // halves)
    n_groups = n_ctx // owners_per_group
    my_group = me // owners_per_group
    part = channels // n_parts

    def load(index, place):
        cols = pl.ds(pl.multiple_of(place * part, LANES), part)
        source = (key_hbm, value_hbm, query_hbm, cot_hbm)[index]
        target = (key, value, query, cot)[index]
        return pltpu.make_async_copy(source.at[:, cols], target.at[:, cols], load_sem.at[index, place])

    rate_load = pltpu.make_async_copy(rate_hbm, rate_ref, param_sem.at[0])
    res_load = pltpu.make_async_copy(res_hbm, res_ref, param_sem.at[1])
    rate_load.start()
    res_load.start()
    for place in range(n_parts):
        for index in range(4):
            load(index, place).start()

    def peer(distance):
        return lax.rem(me + distance, n_ctx)

    def seq_peer(distance):
        return lax.rem(my_seq + distance, n_seq)

    def remote(src, dst, send, recv, target):
        return pltpu.make_async_remote_copy(
            src_ref=src, dst_ref=dst, send_sem=send, recv_sem=recv,
            device_id=target, device_id_type=MESH,
        )

    def owned(ref, owner):
        return ref.at[pl.ds(owner * per_owner, per_owner)]

    def state_copy(owner, slot):
        return remote(owned(state_out, owner), state_in.at[slot], state_send.at[owner], state_recv.at[slot], {"ctx": owner})

    def lag_copy(owner, slot):
        return remote(owned(lag_out, owner), lag_in.at[slot], lag_send.at[owner], lag_recv.at[slot], {"ctx": owner})

    def carry_copy(target, slot):
        return remote(carry_out.at[target], owned(carry_in, slot), carry_send.at[target], carry_recv.at[slot], {"ctx": target})

    def part_copy(target, slot):
        return remote(part_in.at[my_seq], part_in.at[slot], part_send.at[target], part_recv.at[slot], {"seq": target})

    def grad_copy(target, slot):
        return remote(owned(grad_all, me), owned(grad_all, slot), grad_send.at[target], grad_recv.at[slot], {"ctx": target})

    barrier = pltpu.get_barrier_semaphore()
    for distance in range(1, n_ctx):
        pl.semaphore_signal(barrier, inc=1, device_id={"ctx": peer(distance)}, device_id_type=MESH)
    for distance in range(1, n_seq):
        pl.semaphore_signal(barrier, inc=1, device_id={"seq": seq_peer(distance)}, device_id_type=MESH)

    rate_load.wait()
    res_load.wait()
    for block in range(n_blocks):
        cols = slice(block * LANES, (block + 1) * LANES)
        rate = rate_ref[:, cols]
        scale = jnp.sqrt(one_minus_exp(2.0 * rate))
        lam_row[block] = jnp.exp(-rate)
        lam16_row[block] = jnp.exp(-float(steps) * rate)
        weight_row[block] = res_ref[:, cols] * scale
        for half in range(halves):
            rows = slice(half * SUB, (half + 1) * SUB)
            rate_tile[block * halves + half] = rate[rows]
            scale_tile[block * halves + half] = scale[rows]

    to_steps = step_order(length, steps, False)

    def turn(place, _):
        cols = pl.ds(pl.multiple_of(place * part, LANES), part)
        for index in range(4):
            load(index, place).wait()
        key_here, value_here, query_here, cot_here = [
            jnp.dot(to_steps, ref[:, cols], preferred_element_type=F32) for ref in (key, value, query, cot)
        ]
        mixed = key_here * value_here
        adjoint = cot_here * query_here
        for inner in range(part // LANES):
            block = place * (part // LANES) + inner
            lanes = slice(inner * LANES, (inner + 1) * LANES)
            query_p[block] = query_here[:, lanes]
            key_p[block] = key_here[:, lanes]
            value_p[block] = value_here[:, lanes]
            cot_p[block] = cot_here[:, lanes]
            mix_p[block] = mixed[:, lanes]
            adj_p[block] = adjoint[:, lanes]
        return 0

    lax.fori_loop(0, n_parts, turn, 0)

    def wide(ref, block, mode):
        return jnp.broadcast_to(ref[block, pl.ds(mode, 1), :], (SUB, LANES))

    def half_rows(ref, block, half):
        return ref[block, half * SUB:(half + 1) * SUB, :]

    def cut(array):
        return [array[step * SUB:(step + 1) * SUB] for step in range(steps)]

    def states_of(block, inner):
        mix, adj = cut(mix_p[block]), cut(adj_p[block])
        for mode in range(modes):
            lam = wide(lam_row, block, mode)
            last = mix[0]
            first = adj[-1]
            for step in range(1, steps):
                last = last * lam + mix[step]
                first = first * lam + adj[steps - 1 - step]
            up_turn[inner, mode // SUB, mode % SUB] = last
            down_turn[inner, mode // SUB, mode % SUB] = first
        for half in range(halves):
            tile = block * halves + half
            lam16 = half_rows(lam16_row, block, half)
            lasts = [up_turn[inner, half, :, chunk, :] for chunk in range(SUB)]
            firsts = [down_turn[inner, half, :, chunk, :] for chunk in range(SUB)]
            state = lasts[0]
            lag = jnp.zeros_like(state)
            for chunk in range(1, SUB):
                before[tile, chunk] = state
                lag = lag + firsts[chunk] * state
                state = state * lam16 + lasts[chunk]
            state_out[tile, 0] = state
            lag_out[tile] = lag
            state = firsts[-1]
            for chunk in range(SUB - 2, -1, -1):
                after[tile, chunk] = state
                state = state * lam16 + firsts[chunk]
            state_out[tile, 1] = state

    def first_pass(index, _):
        group = lax.rem(my_group + index, n_groups)
        for inner in range(blocks_per_group):
            states_of(group * blocks_per_group + inner, inner)

        @pl.when(index == 1)
        def _():
            pl.semaphore_wait(barrier, n_ctx - 1 + n_seq - 1)

        for inner in range(owners_per_group):
            owner = group * owners_per_group + inner

            @pl.when(owner != me)
            def _():
                state_copy(owner, me).start()

            @pl.when(owner == me)
            def _():
                state_in[me] = state_out[pl.ds(me * per_owner, per_owner)]

        return 0

    lax.fori_loop(1, n_groups + 1, first_pass, 0)

    def chunk_terms(block):
        mix = cut(mix_p[block])
        adj = cut(adj_p[block])
        lam = [lam_row[block, pl.ds(half * SUB, SUB), :] for half in range(halves)]
        power = [weight_row[block, pl.ds(half * SUB, SUB), :] for half in range(halves)]
        taps = []
        for step in range(steps):
            taps.append(jnp.broadcast_to(jnp.sum(sum(power), axis=0, keepdims=True), (SUB, LANES)))
            power = [left * right for left, right in zip(power, lam)]
        for step in range(steps):
            total = taps[0] * mix[step]
            for other in range(step):
                total = total + taps[step - other] * mix[other]
            conv_p[block, pl.ds(step * SUB, SUB), :] = total
            total = taps[0] * adj[step]
            for other in range(step + 1, steps):
                total = total + taps[other - step] * adj[other]
            back_p[block, pl.ds(step * SUB, SUB), :] = total
        sums = [None] * halves
        for lag in range(steps - 1, -1, -1):
            total = adj[lag] * mix[0]
            for step in range(lag + 1, steps):
                total = total + adj[step] * mix[step - lag]
            level = jnp.broadcast_to(jnp.sum(total, axis=0, keepdims=True), (SUB, LANES))
            sums = [level if have is None else have * left + level for have, left in zip(sums, lam)]
        for half in range(halves):
            tile = block * halves + half
            lag_out[tile] = sums[half] + lam[half] * lag_out[tile]

    def second_pass(index, _):
        group = lax.rem(my_group + index, n_groups)
        for inner in range(blocks_per_group):
            chunk_terms(group * blocks_per_group + inner)
        for inner in range(owners_per_group):
            owner = group * owners_per_group + inner

            @pl.when(owner != me)
            def _():
                lag_copy(owner, me).start()

            @pl.when(owner == me)
            def _():
                lag_in[me] = lag_out[pl.ds(me * per_owner, per_owner)]

        return 0

    lax.fori_loop(1, n_groups // 2 + 1, second_pass, 0)

    for distance in range(1, n_ctx):
        source = peer(n_ctx - distance)
        state_copy(source, source).wait_recv()
    for place in range(per_owner):
        rate = rate_tile[me * per_owner + place]
        lam = jnp.exp(-rate)
        hop = jnp.exp(-float(length) * rate)
        carried = jnp.zeros((SUB, LANES), F32)
        cross = jnp.zeros((SUB, LANES), F32)
        for source in range(n_ctx):
            carry_out[source, place, 0] = carried
            cross = cross + carried * state_in[source, place, 1]
            carried = carried * hop + state_in[source, place, 0]
        part_in[my_seq, place] = lam * cross
        carried = jnp.zeros((SUB, LANES), F32)
        for source in range(n_ctx - 1, -1, -1):
            carry_out[source, place, 1] = carried
            carried = carried * hop + state_in[source, place, 1]
    for distance in range(1, n_ctx):
        carry_copy(peer(distance), me).start()
    carry_in[pl.ds(me * per_owner, per_owner)] = carry_out[me]

    lax.fori_loop(n_groups // 2 + 1, n_groups + 1, second_pass, 0)

    def finish(block, inner):
        cols = columns_of(block)
        for half in range(halves):
            tile = block * halves + half
            lam16 = half_rows(lam16_row, block, half)
            lead = half_rows(lam_row, block, half) * half_rows(weight_row, block, half)
            state = carry_in[tile, 0]
            for chunk in range(SUB):
                up_turn[inner, half, chunk] = lead * (state + before[tile, chunk] if chunk else state)
                state = state * lam16
            state = carry_in[tile, 1]
            for chunk in range(SUB - 1, -1, -1):
                down_turn[inner, half, chunk] = lead * (state + after[tile, chunk] if chunk < SUB - 1 else state)
                state = state * lam16
        conv = cut(conv_p[block])
        back = cut(back_p[block])
        for mode in range(modes):
            lam = wide(lam_row, block, mode)
            term = up_turn[inner, mode // SUB, :, mode % SUB, :]
            other = down_turn[inner, mode // SUB, :, mode % SUB, :]
            for step in range(steps):
                conv[step] = conv[step] + term
                back[steps - 1 - step] = back[steps - 1 - step] + other
                if step + 1 < steps:
                    term = term * lam
                    other = other * lam
        conv = jnp.concatenate(conv, axis=0)
        back = jnp.concatenate(back, axis=0)
        out[:, cols] = (query_p[block] * conv).astype(jnp.bfloat16)
        grad_query[:, cols] = (cot_p[block] * conv).astype(jnp.bfloat16)
        grad_key[:, cols] = (value_p[block] * back).astype(jnp.bfloat16)
        grad_value[:, cols] = (key_p[block] * back).astype(jnp.bfloat16)

    def last_pass(index, _):
        group = lax.rem(my_group + n_groups - index, n_groups)
        for inner in range(owners_per_group):
            owner = group * owners_per_group + inner

            @pl.when(owner != me)
            def _():
                carry_copy(owner, owner).wait_recv()

        for inner in range(blocks_per_group):
            finish(group * blocks_per_group + inner, inner)

        @pl.when(index == 0)
        def _():
            for distance in range(1, n_ctx):
                source = peer(n_ctx - distance)
                lag_copy(source, source).wait_recv()
            for place in range(per_owner):
                total = part_in[my_seq, place]
                for source in range(n_ctx):
                    total = total + lag_in[source, place]
                part_in[my_seq, place] = total * scale_tile[me * per_owner + place]
            for distance in range(1, n_seq):
                part_copy(seq_peer(distance), my_seq).start()

        @pl.when(index == n_groups // 2)
        def _():
            for distance in range(1, n_seq):
                source = seq_peer(n_seq - distance)
                part_copy(source, source).wait_recv()
            for place in range(per_owner):
                total = part_in[0, place]
                for source in range(1, n_seq):
                    total = total + part_in[source, place]
                grad_all[me * per_owner + place] = total * (1.0 / (length * n_ctx * n_seq))
            for distance in range(1, n_ctx):
                grad_copy(peer(distance), me).start()

        return 0

    lax.fori_loop(0, n_groups, last_pass, 0)

    for distance in range(1, n_ctx):
        source = peer(n_ctx - distance)
        grad_copy(source, source).wait_recv()
    for block in range(n_blocks):
        for half in range(halves):
            grad_res[half * SUB:(half + 1) * SUB, block * LANES:(block + 1) * LANES] = grad_all[block * halves + half]

    for distance in range(1, n_ctx):
        target = peer(distance)
        state_copy(target, me).wait_send()
        lag_copy(target, me).wait_send()
        carry_copy(target, me).wait_send()
        grad_copy(target, me).wait_send()
    for distance in range(1, n_seq):
        part_copy(seq_peer(distance), my_seq).wait_send()


def writer(out_p, grad_query_p, grad_key_p, grad_value_p, grad_res, out, grad_query, grad_key, grad_value, grad_res_hbm, *scratch):
    stage, sems, grad_sem = scratch[:4], scratch[4], scratch[5]
    length, channels = out_p.shape
    n_parts = sems.shape[1]
    part = channels // n_parts
    whole = pltpu.make_async_copy(grad_res, grad_res_hbm, grad_sem)
    whole.start()
    to_tokens = step_order(length, length // SUB, True)
    copies = []
    for place in range(n_parts):
        cols = slice(place * part, (place + 1) * part)
        for index, (source, target) in enumerate(
            zip((out_p, grad_query_p, grad_key_p, grad_value_p), (out, grad_query, grad_key, grad_value))
        ):
            stage[index][:, cols] = jnp.dot(to_tokens, source[:, cols], preferred_element_type=F32).astype(jnp.bfloat16)
            copies.append(pltpu.make_async_copy(stage[index].at[:, cols], target.at[:, cols], sems.at[index, place]))
            copies[-1].start()
    for copy in copies:
        copy.wait()
    whole.wait()


def on_device(n_ctx, n_seq, query_input, key_input, value_input, cotangent, residues, decay_rates):
    _, length, channels = query_input.shape
    modes = residues.shape[1]
    n_blocks = channels // LANES
    halves = modes // SUB
    n_tiles = n_blocks * halves
    per_owner = n_tiles // n_ctx

    def rows():
        return pltpu.VMEM((n_blocks, length, LANES), F32)

    def tiles(*leading):
        return pltpu.VMEM(leading + (SUB, LANES), F32)

    signal = jax.ShapeDtypeStruct((length, channels), jnp.bfloat16)
    vmem = pl.BlockSpec(memory_space=pltpu.VMEM)
    hbm = pl.BlockSpec(memory_space=pltpu.HBM)
    n_parts = 4
    wide_rows = [pltpu.VMEM((length, channels), jnp.bfloat16) for _ in range(4)]
    results = pl.pallas_call(
        functools.partial(kernel, n_ctx, n_seq, n_parts),
        out_shape=[signal] * 4 + [jax.ShapeDtypeStruct((modes, channels), F32)],
        in_specs=[hbm] * 6,
        out_specs=[vmem] * 5,
        scratch_shapes=wide_rows
        + [pltpu.VMEM((modes, channels), F32) for _ in range(2)]
        + [rows() for _ in range(8)]
        + [tiles(n_tiles, SUB), tiles(n_tiles, SUB)]
        + [tiles(max(1, per_owner // halves), halves, SUB) for _ in range(2)]
        + [pltpu.VMEM((n_blocks, modes, LANES), F32) for _ in range(3)]
        + [tiles(n_tiles), tiles(n_tiles)]
        + [
            tiles(n_tiles, 2), tiles(n_ctx, per_owner, 2),
            tiles(n_ctx, per_owner, 2), tiles(n_tiles, 2),
            tiles(n_tiles), tiles(n_ctx, per_owner),
            tiles(n_seq, per_owner), tiles(n_tiles),
        ]
        + [pltpu.SemaphoreType.DMA((n_ctx,)) for _ in range(6)]
        + [pltpu.SemaphoreType.DMA((n_seq,)) for _ in range(2)]
        + [pltpu.SemaphoreType.DMA((n_ctx,)) for _ in range(2)]
        + [pltpu.SemaphoreType.DMA((4, n_parts)), pltpu.SemaphoreType.DMA((2,))],
        compiler_params=pltpu.CompilerParams(
            collective_id=0, has_side_effects=True, vmem_limit_bytes=829 * 64 * 1024
        ),
        cost_estimate=pl.CostEstimate(flops=100_000_000, bytes_accessed=4_500_000, transcendentals=1_000_000),
        name="modal_states",
    )(query_input[0], key_input[0], value_input[0], cotangent[0], residues.T, decay_rates.T)
    results = pl.pallas_call(
        writer,
        out_shape=[signal] * 4 + [jax.ShapeDtypeStruct((modes, channels), F32)],
        in_specs=[vmem] * 5,
        out_specs=[hbm] * 5,
        scratch_shapes=wide_rows + [pltpu.SemaphoreType.DMA((4, n_parts)), pltpu.SemaphoreType.DMA],
        compiler_params=pltpu.CompilerParams(vmem_limit_bytes=16 * 1024 * 1024),
        cost_estimate=pl.CostEstimate(flops=300_000_000, bytes_accessed=4_500_000, transcendentals=0),
        name="token_order",
    )(*results)
    return tuple(array[None] for array in results[:4]) + (results[4].T,)


def solution(mesh):
    wide = P("seq", "ctx", None)
    return jax.shard_map(
        functools.partial(on_device, mesh.shape["ctx"], mesh.shape["seq"]),
        mesh=mesh,
        in_specs=(wide, wide, wide, wide, P(), P()),
        out_specs=(wide, wide, wide, wide, P()),
        check_vma=False,
    )
```

```python
import functools

import jax
import jax.numpy as jnp
from jax import lax
from jax.experimental import pallas as pl
from jax.experimental.pallas import tpu as pltpu
from jax.sharding import PartitionSpec as P

SUB = 8
LANES = 128
MESH = pl.DeviceIdType.MESH
F32 = jnp.float32


def one_minus_exp(u):
    total = jnp.ones_like(u)
    for order in range(8, 1, -1):
        total = 1.0 - (u / order) * total
    return u * total


def columns_of(block):
    return pl.ds(pl.multiple_of(block * LANES, LANES), LANES)


def step_order(length, steps, inverse):
    row = lax.broadcasted_iota(jnp.int32, (length, length), 0)
    col = lax.broadcasted_iota(jnp.int32, (length, length), 1)
    if inverse:
        row, col = col, row
    return jnp.where(col == steps * (row % SUB) + row // SUB, 1.0, 0.0).astype(jnp.bfloat16)


def kernel(
    n_ctx, n_seq, n_parts, query_hbm, key_hbm, value_hbm, cot_hbm, res_hbm, rate_hbm,
    result_hbm, grad_all,
    query, key, value, cot, res_ref, rate_ref, result,
    query_p, key_p, value_p, cot_p, mix_p, adj_p, conv_p, back_p, before, after, up_turn, down_turn,
    lam_row, lam16_row, weight_row, rate_tile, scale_tile,
    state_out, state_in, carry_out, carry_in, lag_out, lag_in, part_in, grad_own,
    state_send, state_recv, carry_send, carry_recv, lag_send, lag_recv,
    part_send, part_recv, grad_send, grad_recv, load_sem, param_sem, store_sem, own_sem,
):
    me = lax.axis_index("ctx")
    my_seq = lax.axis_index("seq")
    length, channels = query.shape
    modes = res_ref.shape[0]
    steps = length // SUB
    n_blocks = channels // LANES
    halves = modes // SUB
    n_tiles = n_blocks * halves
    per_owner = n_tiles // n_ctx
    owners_per_group = max(1, halves // per_owner)
    blocks_per_group = max(1, per_owner // halves)
    n_groups = n_ctx // owners_per_group
    my_group = me // owners_per_group
    part = channels // n_parts

    def load(index, place):
        cols = pl.ds(pl.multiple_of(place * part, LANES), part)
        source = (key_hbm, value_hbm, query_hbm, cot_hbm)[index]
        target = (key, value, query, cot)[index]
        return pltpu.make_async_copy(source.at[:, cols], target.at[:, cols], load_sem.at[index, place])

    rate_load = pltpu.make_async_copy(rate_hbm, rate_ref, param_sem.at[0])
    res_load = pltpu.make_async_copy(res_hbm, res_ref, param_sem.at[1])
    rate_load.start()
    res_load.start()
    for place in range(n_parts):
        for index in range(4):
            load(index, place).start()

    def peer(distance):
        return lax.rem(me + distance, n_ctx)

    def seq_peer(distance):
        return lax.rem(my_seq + distance, n_seq)

    def remote(src, dst, send, recv, target):
        return pltpu.make_async_remote_copy(
            src_ref=src, dst_ref=dst, send_sem=send, recv_sem=recv,
            device_id=target, device_id_type=MESH,
        )

    def owned(ref, owner):
        return ref.at[pl.ds(owner * per_owner, per_owner)]

    def state_copy(owner, slot):
        return remote(owned(state_out, owner), state_in.at[slot], state_send.at[owner], state_recv.at[slot], {"ctx": owner})

    def lag_copy(owner, slot):
        return remote(owned(lag_out, owner), lag_in.at[slot], lag_send.at[owner], lag_recv.at[slot], {"ctx": owner})

    def carry_copy(target, slot):
        return remote(carry_out.at[target], owned(carry_in, slot), carry_send.at[target], carry_recv.at[slot], {"ctx": target})

    def part_copy(target, slot):
        return remote(part_in.at[my_seq], part_in.at[slot], part_send.at[target], part_recv.at[slot], {"seq": target})

    def grad_copy(target, slot):
        return remote(grad_own, owned(grad_all, slot), grad_send.at[target], grad_recv.at[slot], {"ctx": target})

    barrier = pltpu.get_barrier_semaphore()
    for distance in range(1, n_ctx):
        pl.semaphore_signal(barrier, inc=1, device_id={"ctx": peer(distance)}, device_id_type=MESH)
    for distance in range(1, n_seq):
        pl.semaphore_signal(barrier, inc=1, device_id={"seq": seq_peer(distance)}, device_id_type=MESH)

    rate_load.wait()
    res_load.wait()
    for block in range(n_blocks):
        cols = slice(block * LANES, (block + 1) * LANES)
        rate = rate_ref[:, cols]
        scale = jnp.sqrt(one_minus_exp(2.0 * rate))
        lam_row[block] = jnp.exp(-rate)
        lam16_row[block] = jnp.exp(-float(steps) * rate)
        weight_row[block] = res_ref[:, cols] * scale
        for half in range(halves):
            rows = slice(half * SUB, (half + 1) * SUB)
            rate_tile[block * halves + half] = rate[rows]
            scale_tile[block * halves + half] = scale[rows]

    to_steps = step_order(length, steps, False)

    def turn(place, _):
        cols = pl.ds(pl.multiple_of(place * part, LANES), part)
        for index in range(4):
            load(index, place).wait()
        key_here, value_here, query_here, cot_here = [
            jnp.dot(to_steps, ref[:, cols], preferred_element_type=F32) for ref in (key, value, query, cot)
        ]
        mixed = key_here * value_here
        adjoint = cot_here * query_here
        for inner in range(part // LANES):
            block = place * (part // LANES) + inner
            lanes = slice(inner * LANES, (inner + 1) * LANES)
            query_p[block] = query_here[:, lanes]
            key_p[block] = key_here[:, lanes]
            value_p[block] = value_here[:, lanes]
            cot_p[block] = cot_here[:, lanes]
            mix_p[block] = mixed[:, lanes]
            adj_p[block] = adjoint[:, lanes]
        return 0

    lax.fori_loop(0, n_parts, turn, 0)

    def wide(ref, block, mode):
        return jnp.broadcast_to(ref[block, pl.ds(mode, 1), :], (SUB, LANES))

    def half_rows(ref, block, half):
        return ref[block, half * SUB:(half + 1) * SUB, :]

    def rows_at(ref, block, step):
        return ref[block, step * SUB:(step + 1) * SUB, :]

    def tree(terms):
        while len(terms) > 1:
            terms = [sum(terms[place:place + 2][1:], terms[place]) for place in range(0, len(terms), 2)]
        return terms[0]

    def cut(array):
        return [array[step * SUB:(step + 1) * SUB] for step in range(steps)]

    def states_of(block, inner):
        for half in range(halves):
            lams = [wide(lam_row, block, half * SUB + mode) for mode in range(SUB)]
            lasts = [rows_at(mix_p, block, 0)] * SUB
            firsts = [rows_at(adj_p, block, steps - 1)] * SUB
            for step in range(1, steps):
                mix, adj = rows_at(mix_p, block, step), rows_at(adj_p, block, steps - 1 - step)
                lasts = [have * lam + mix for have, lam in zip(lasts, lams)]
                firsts = [have * lam + adj for have, lam in zip(firsts, lams)]
            for mode in range(SUB):
                up_turn[inner, half, mode] = lasts[mode]
                down_turn[inner, half, mode] = firsts[mode]
        for half in range(halves):
            tile = block * halves + half
            lam16 = half_rows(lam16_row, block, half)
            lasts = [up_turn[inner, half, :, chunk, :] for chunk in range(SUB)]
            firsts = [down_turn[inner, half, :, chunk, :] for chunk in range(SUB)]
            state = lasts[0]
            lag = jnp.zeros_like(state)
            for chunk in range(1, SUB):
                before[tile, chunk] = state
                lag = lag + firsts[chunk] * state
                state = state * lam16 + lasts[chunk]
            state_out[tile, 0] = state
            lag_out[tile] = lag
            state = firsts[-1]
            for chunk in range(SUB - 2, -1, -1):
                after[tile, chunk] = state
                state = state * lam16 + firsts[chunk]
            state_out[tile, 1] = state

    def first_pass(index, _):
        group = lax.rem(my_group + index, n_groups)
        for inner in range(blocks_per_group):
            states_of(group * blocks_per_group + inner, inner)

        @pl.when(index == 1)
        def _():
            pl.semaphore_wait(barrier, n_ctx - 1 + n_seq - 1)

        for inner in range(owners_per_group):
            owner = group * owners_per_group + inner

            @pl.when(owner != me)
            def _():
                state_copy(owner, me).start()

            @pl.when(owner == me)
            def _():
                state_in[me] = state_out[pl.ds(me * per_owner, per_owner)]

        return 0

    lax.fori_loop(1, n_groups + 1, first_pass, 0)

    def chunk_terms(block):
        mix = cut(mix_p[block])
        adj = cut(adj_p[block])
        lam = [lam_row[block, pl.ds(half * SUB, SUB), :] for half in range(halves)]
        power = [weight_row[block, pl.ds(half * SUB, SUB), :] for half in range(halves)]
        taps = []
        for step in range(steps):
            taps.append(jnp.broadcast_to(jnp.sum(sum(power), axis=0, keepdims=True), (SUB, LANES)))
            power = [left * right for left, right in zip(power, lam)]
        totals = [taps[0] * rows for rows in mix]
        for lag in range(1, steps):
            for step in range(lag, steps):
                totals[step] = totals[step] + taps[lag] * mix[step - lag]
        for step in range(steps):
            conv_p[block, step * SUB:(step + 1) * SUB, :] = totals[step]
        totals = [taps[0] * rows for rows in adj]
        for lag in range(1, steps):
            for step in range(steps - lag):
                totals[step] = totals[step] + taps[lag] * adj[step + lag]
        for step in range(steps):
            back_p[block, step * SUB:(step + 1) * SUB, :] = totals[step]
        totals = [rows * mix[0] for rows in adj]
        for step in range(1, steps):
            for lag in range(steps - step):
                totals[lag] = totals[lag] + adj[step + lag] * mix[step]
        levels = [jnp.broadcast_to(jnp.sum(total, axis=0, keepdims=True), (SUB, LANES)) for total in totals]
        sums = [levels[-1]] * halves
        for level in levels[-2::-1]:
            sums = [have * left + level for have, left in zip(sums, lam)]
        for half in range(halves):
            tile = block * halves + half
            lag_out[tile] = sums[half] + lam[half] * lag_out[tile]

    def second_pass(index, _):
        group = lax.rem(my_group + index, n_groups)
        for inner in range(blocks_per_group):
            chunk_terms(group * blocks_per_group + inner)
        for inner in range(owners_per_group):
            owner = group * owners_per_group + inner

            @pl.when(owner != me)
            def _():
                lag_copy(owner, me).start()

            @pl.when(owner == me)
            def _():
                lag_in[me] = lag_out[pl.ds(me * per_owner, per_owner)]

        return 0

    lax.fori_loop(1, n_groups // 2 + 1, second_pass, 0)

    for distance in range(1, n_ctx):
        source = peer(n_ctx - distance)
        state_copy(source, source).wait_recv()
    for place in range(per_owner):
        rate = rate_tile[me * per_owner + place]
        lam = jnp.exp(-rate)
        hop = jnp.exp(-float(length) * rate)
        carried = jnp.zeros((SUB, LANES), F32)
        cross = jnp.zeros((SUB, LANES), F32)
        for source in range(n_ctx):
            carry_out[source, place, 0] = carried
            cross = cross + carried * state_in[source, place, 1]
            carried = carried * hop + state_in[source, place, 0]
        part_in[my_seq, place] = lam * cross
        carried = jnp.zeros((SUB, LANES), F32)
        for source in range(n_ctx - 1, -1, -1):
            carry_out[source, place, 1] = carried
            carried = carried * hop + state_in[source, place, 1]
    for distance in range(1, n_ctx):
        carry_copy(peer(distance), me).start()
    carry_in[pl.ds(me * per_owner, per_owner)] = carry_out[me]

    lax.fori_loop(n_groups // 2 + 1, n_groups + 1, second_pass, 0)

    def finish(block, inner):
        cols = columns_of(block)
        for half in range(halves):
            tile = block * halves + half
            lam16 = half_rows(lam16_row, block, half)
            lead = half_rows(lam_row, block, half) * half_rows(weight_row, block, half)
            state = carry_in[tile, 0]
            for chunk in range(SUB):
                up_turn[inner, half, chunk] = lead * (state + before[tile, chunk] if chunk else state)
                state = state * lam16
            state = carry_in[tile, 1]
            for chunk in range(SUB - 1, -1, -1):
                down_turn[inner, half, chunk] = lead * (state + after[tile, chunk] if chunk < SUB - 1 else state)
                state = state * lam16
        lams = [wide(lam_row, block, mode) for mode in range(modes)]

        def put(place, step, factor, pair):
            rows = pl.ds(step * SUB, 2 * SUB)
            target = slice(place * length + step * SUB, place * length + (step + 2) * SUB)
            result[target, cols] = (factor[block, rows, :] * pair).astype(jnp.bfloat16)

        terms = [up_turn[inner, mode // SUB, :, mode % SUB, :] for mode in range(modes)]
        sums = []
        for step in range(steps):
            sums.append(rows_at(conv_p, block, step) + tree(terms))
            terms = [term * lam for term, lam in zip(terms, lams)]
            if step % 2:
                pair = jnp.concatenate(sums, axis=0)
                put(0, step - 1, query_p, pair)
                put(1, step - 1, cot_p, pair)
                sums = []
        terms = [down_turn[inner, mode // SUB, :, mode % SUB, :] for mode in range(modes)]
        for step in range(steps - 1, -1, -1):
            sums.insert(0, rows_at(back_p, block, step) + tree(terms))
            terms = [term * lam for term, lam in zip(terms, lams)]
            if step % 2 == 0:
                pair = jnp.concatenate(sums, axis=0)
                put(2, step, value_p, pair)
                put(3, step, key_p, pair)
                sums = []

    own_copy = pltpu.make_async_copy(grad_own, owned(grad_all, me), own_sem)

    def store(group):
        width = blocks_per_group * LANES
        cols = pl.ds(pl.multiple_of(group * width, LANES), width)
        return pltpu.make_async_copy(result.at[:, cols], result_hbm.at[:, cols], store_sem.at[group])

    def last_pass(index, _):
        group = lax.rem(my_group + n_groups - index, n_groups)
        for inner in range(owners_per_group):
            owner = group * owners_per_group + inner

            @pl.when(owner != me)
            def _():
                carry_copy(owner, owner).wait_recv()

        for inner in range(blocks_per_group):
            finish(group * blocks_per_group + inner, inner)
        store(group).start()

        @pl.when(index == 0)
        def _():
            for distance in range(1, n_ctx):
                source = peer(n_ctx - distance)
                lag_copy(source, source).wait_recv()
            for place in range(per_owner):
                total = part_in[my_seq, place]
                for source in range(n_ctx):
                    total = total + lag_in[source, place]
                part_in[my_seq, place] = total * scale_tile[me * per_owner + place]
            for distance in range(1, n_seq):
                part_copy(seq_peer(distance), my_seq).start()

        @pl.when(index == n_groups // 2)
        def _():
            for distance in range(1, n_seq):
                source = seq_peer(n_seq - distance)
                part_copy(source, source).wait_recv()
            for place in range(per_owner):
                total = part_in[0, place]
                for source in range(1, n_seq):
                    total = total + part_in[source, place]
                grad_own[place] = total * (1.0 / (length * n_ctx * n_seq))
            for distance in range(1, n_ctx):
                grad_copy(peer(distance), me).start()
            own_copy.start()

        return 0

    lax.fori_loop(0, n_groups, last_pass, 0)

    for distance in range(1, n_ctx):
        source = peer(n_ctx - distance)
        grad_copy(source, source).wait_recv()
    own_copy.wait()
    for group in range(n_groups):
        store(group).wait()
    for distance in range(1, n_ctx):
        target = peer(distance)
        state_copy(target, me).wait_send()
        lag_copy(target, me).wait_send()
        carry_copy(target, me).wait_send()
        grad_copy(target, me).wait_send()
    for distance in range(1, n_seq):
        part_copy(seq_peer(distance), my_seq).wait_send()


def writer(
    result, grad_all, out, grad_query, grad_key, grad_value, grad_res,
    stage, turned, grad_tiles, grad_rows, load_sem, store_sem, grad_sem,
):
    length, channels = out.shape
    n_parts = load_sem.shape[1]
    part = channels // n_parts
    n_tiles = grad_all.shape[0]
    halves = grad_res.shape[0] // SUB
    targets = (out, grad_query, grad_key, grad_value)

    def place_of(index, place):
        return slice(index * length, (index + 1) * length), slice(place * part, (place + 1) * part)

    loads, stores = {}, []
    for place in range(n_parts):
        for index in range(4):
            where = place_of(index, place)
            loads[index, place] = pltpu.make_async_copy(result.at[where], stage.at[where], load_sem.at[index, place])
            loads[index, place].start()
    grad_load = pltpu.make_async_copy(grad_all, grad_tiles, grad_sem.at[0])
    grad_load.start()
    to_tokens = step_order(length, length // SUB, True)
    for place in range(n_parts):
        for index in range(4):
            where = place_of(index, place)
            loads[index, place].wait()
            turned[where] = jnp.dot(to_tokens, stage[where], preferred_element_type=F32).astype(jnp.bfloat16)
            stores.append(pltpu.make_async_copy(turned.at[where], targets[index].at[:, where[1]], store_sem.at[index, place]))
            stores[-1].start()
    grad_load.wait()
    for tile in range(n_tiles):
        block, half = divmod(tile, halves)
        grad_rows[half * SUB:(half + 1) * SUB, block * LANES:(block + 1) * LANES] = grad_tiles[tile]
    stores.append(pltpu.make_async_copy(grad_rows, grad_res, grad_sem.at[1]))
    stores[-1].start()
    for copy in stores:
        copy.wait()


def on_device(n_ctx, n_seq, query_input, key_input, value_input, cotangent, residues, decay_rates):
    _, length, channels = query_input.shape
    modes = residues.shape[1]
    n_blocks = channels // LANES
    halves = modes // SUB
    n_tiles = n_blocks * halves
    per_owner = n_tiles // n_ctx

    def rows():
        return pltpu.VMEM((n_blocks, length, LANES), F32)

    def tiles(*leading):
        return pltpu.VMEM(leading + (SUB, LANES), F32)

    signal = jax.ShapeDtypeStruct((length, channels), jnp.bfloat16)
    hbm = pl.BlockSpec(memory_space=pltpu.HBM)
    n_parts = 4
    wide_rows = [pltpu.VMEM((length, channels), jnp.bfloat16) for _ in range(4)]
    results = pl.pallas_call(
        functools.partial(kernel, n_ctx, n_seq, n_parts),
        out_shape=[jax.ShapeDtypeStruct((4 * length, channels), jnp.bfloat16), jax.ShapeDtypeStruct((n_tiles, SUB, LANES), F32)],
        in_specs=[hbm] * 6,
        out_specs=[hbm] * 2,
        scratch_shapes=wide_rows
        + [pltpu.VMEM((modes, channels), F32) for _ in range(2)]
        + [pltpu.VMEM((4 * length, channels), jnp.bfloat16)]
        + [rows() for _ in range(8)]
        + [tiles(n_tiles, SUB), tiles(n_tiles, SUB)]
        + [tiles(max(1, per_owner // halves), halves, SUB) for _ in range(2)]
        + [pltpu.VMEM((n_blocks, modes, LANES), F32) for _ in range(3)]
        + [tiles(n_tiles), tiles(n_tiles)]
        + [
            tiles(n_tiles, 2), tiles(n_ctx, per_owner, 2),
            tiles(n_ctx, per_owner, 2), tiles(n_tiles, 2),
            tiles(n_tiles), tiles(n_ctx, per_owner),
            tiles(n_seq, per_owner), tiles(per_owner),
        ]
        + [pltpu.SemaphoreType.DMA((n_ctx,)) for _ in range(6)]
        + [pltpu.SemaphoreType.DMA((n_seq,)) for _ in range(2)]
        + [pltpu.SemaphoreType.DMA((n_ctx,)) for _ in range(2)]
        + [pltpu.SemaphoreType.DMA((4, n_parts)), pltpu.SemaphoreType.DMA((2,))]
        + [pltpu.SemaphoreType.DMA((n_ctx,)), pltpu.SemaphoreType.DMA],
        compiler_params=pltpu.CompilerParams(
            collective_id=0, has_side_effects=True, vmem_limit_bytes=60 * 1024 * 1024
        ),
        cost_estimate=pl.CostEstimate(flops=100_000_000, bytes_accessed=4_500_000, transcendentals=1_000_000),
        name="modal_states",
    )(query_input[0], key_input[0], value_input[0], cotangent[0], residues.T, decay_rates.T)
    results = pl.pallas_call(
        writer,
        out_shape=[signal] * 4 + [jax.ShapeDtypeStruct((modes, channels), F32)],
        in_specs=[hbm] * 2,
        out_specs=[hbm] * 5,
        scratch_shapes=[pltpu.VMEM((4 * length, channels), jnp.bfloat16) for _ in range(2)]
        + [tiles(n_tiles), pltpu.VMEM((modes, channels), F32)]
        + [pltpu.SemaphoreType.DMA((4, n_parts)) for _ in range(2)]
        + [pltpu.SemaphoreType.DMA((2,))],
        compiler_params=pltpu.CompilerParams(vmem_limit_bytes=60 * 1024 * 1024),
        cost_estimate=pl.CostEstimate(flops=300_000_000, bytes_accessed=4_500_000, transcendentals=0),
        name="token_order",
    )(*results)
    return tuple(array[None] for array in results[:4]) + (results[4].T,)


def solution(mesh):
    wide = P("seq", "ctx", None)
    return jax.shard_map(
        functools.partial(on_device, mesh.shape["ctx"], mesh.shape["seq"]),
        mesh=mesh,
        in_specs=(wide, wide, wide, wide, P(), P()),
        out_specs=(wide, wide, wide, wide, P()),
        check_vma=False,
    )
```

```python
import functools

import jax
import jax.numpy as jnp
from jax import lax
from jax.experimental import pallas as pl
from jax.experimental.pallas import tpu as pltpu
from jax.sharding import PartitionSpec as P

SUB = 8
LANES = 128
LOCAL = 4
MESH = pl.DeviceIdType.MESH
F32 = jnp.float32


def one_minus_exp(u):
    total = jnp.ones_like(u)
    for order in range(8, 1, -1):
        total = 1.0 - (u / order) * total
    return u * total


def columns_of(block):
    return pl.ds(pl.multiple_of(block * LANES, LANES), LANES)


def step_order(length, steps, inverse):
    row = lax.broadcasted_iota(jnp.int32, (length, length), 0)
    col = lax.broadcasted_iota(jnp.int32, (length, length), 1)
    if inverse:
        row, col = col, row
    return jnp.where(col == steps * (row % SUB) + row // SUB, 1.0, 0.0).astype(jnp.bfloat16)


def kernel(
    n_ctx, n_seq, n_parts, query_hbm, key_hbm, value_hbm, cot_hbm, param_ref,
    out, grad_query, grad_key, grad_value, grad_all,
    query, key, value, cot,
    query_p, key_p, value_p, cot_p, mix_p, adj_p, conv_p, back_p, before, after, up_turn, down_turn,
    lam_row, lam16_row, weight_row, rate_tile, scale_tile,
    state_out, state_in, carry_out, carry_in, hop_up, hop_down, hop_in,
    cross_out, cross_in, lag_out, lag_in, part_in, grad_own,
    state_send, state_recv, carry_send, carry_recv, hop_send, hop_recv, cross_send, cross_recv,
    lag_send, lag_recv, grad_send, grad_recv, part_send, part_recv, load_sem, own_sem,
):
    me = lax.axis_index("ctx")
    my_seq = lax.axis_index("seq")
    length, channels = query.shape
    modes = param_ref.shape[0] // 2
    steps = length // SUB
    n_blocks = channels // LANES
    halves = modes // SUB
    n_tiles = n_blocks * halves
    n_groups = n_ctx // LOCAL
    my_group, my_local = me // LOCAL, lax.rem(me, LOCAL)
    per_owner = n_tiles // LOCAL
    per_sum = per_owner // n_groups
    owner_blocks = per_owner // halves
    piece_blocks = max(1, owner_blocks // 2)
    owner_pieces = owner_blocks // piece_blocks
    piece_tiles = piece_blocks * halves
    n_pieces = n_blocks // piece_blocks
    part = channels // n_parts

    def load(index, place):
        cols = pl.ds(pl.multiple_of(place * part, LANES), part)
        source = (key_hbm, value_hbm, query_hbm, cot_hbm)[index]
        target = (key, value, query, cot)[index]
        return pltpu.make_async_copy(source.at[:, cols], target.at[:, cols], load_sem.at[index, place])

    for place in range(n_parts):
        for index in range(4):
            load(index, place).start()

    def peer(distance):
        return lax.rem(me + distance, n_ctx)

    def seq_peer(distance):
        return lax.rem(my_seq + distance, n_seq)

    def remote(src, dst, send, recv, target):
        return pltpu.make_async_remote_copy(
            src_ref=src, dst_ref=dst, send_sem=send, recv_sem=recv,
            device_id=target, device_id_type=MESH,
        )

    def piece_of(ref, piece):
        return ref.at[pl.ds(piece * piece_tiles, piece_tiles)]

    def sum_start(owner):
        return lax.rem(owner, LOCAL) * per_owner + owner // LOCAL * per_sum

    def summed(ref, owner):
        return ref.at[pl.ds(sum_start(owner), per_sum)]

    def state_copy(owner, place, slot):
        return remote(
            piece_of(state_out, owner * owner_pieces + place), piece_of(state_in.at[slot], place),
            state_send.at[owner, place], state_recv.at[slot, place], {"ctx": my_group * LOCAL + owner},
        )

    def carry_copy(target, place, slot):
        return remote(
            piece_of(carry_out.at[target], place), piece_of(carry_in, slot * owner_pieces + place),
            carry_send.at[target, place], carry_recv.at[slot, place], {"ctx": my_group * LOCAL + target},
        )

    def hop_copy(source, target, slot):
        return remote(source, hop_in.at[slot], hop_send.at[target], hop_recv.at[slot], {"ctx": target * LOCAL + my_local})

    def cross_copy(target, slot):
        return remote(
            cross_out.at[pl.ds(target * per_sum, per_sum)], cross_in.at[slot],
            cross_send.at[target], cross_recv.at[slot], {"ctx": target * LOCAL + my_local},
        )

    def lag_copy(owner, slot):
        return remote(summed(lag_out, owner), lag_in.at[slot], lag_send.at[owner], lag_recv.at[slot], {"ctx": owner})

    def part_copy(target, slot):
        return remote(part_in.at[my_seq], part_in.at[slot], part_send.at[target], part_recv.at[slot], {"seq": target})

    def grad_copy(target, slot):
        return remote(grad_own, summed(grad_all, slot), grad_send.at[target], grad_recv.at[slot], {"ctx": target})

    barrier = pltpu.get_barrier_semaphore()
    for distance in range(1, n_ctx):
        pl.semaphore_signal(barrier, inc=1, device_id={"ctx": peer(distance)}, device_id_type=MESH)
    for distance in range(1, n_seq):
        pl.semaphore_signal(barrier, inc=1, device_id={"seq": seq_peer(distance)}, device_id_type=MESH)

    for block in range(n_blocks):
        cols = slice(block * LANES, (block + 1) * LANES)
        rate = param_ref[:modes, cols]
        scale = jnp.sqrt(one_minus_exp(2.0 * rate))
        lam_row[block] = jnp.exp(-rate)
        lam16_row[block] = jnp.exp(-float(steps) * rate)
        weight_row[block] = param_ref[modes:, cols] * scale
        for half in range(halves):
            rows = slice(half * SUB, (half + 1) * SUB)
            rate_tile[block * halves + half] = rate[rows]
            scale_tile[block * halves + half] = scale[rows]

    to_steps = step_order(length, steps, False)

    def turn(place, _):
        cols = pl.ds(pl.multiple_of(place * part, LANES), part)
        for index in range(4):
            load(index, place).wait()
        key_here, value_here, query_here, cot_here = [
            jnp.dot(to_steps, ref[:, cols], preferred_element_type=F32) for ref in (key, value, query, cot)
        ]
        mixed = key_here * value_here
        adjoint = cot_here * query_here
        for inner in range(part // LANES):
            block = place * (part // LANES) + inner
            lanes = slice(inner * LANES, (inner + 1) * LANES)
            query_p[block] = query_here[:, lanes]
            key_p[block] = key_here[:, lanes]
            value_p[block] = value_here[:, lanes]
            cot_p[block] = cot_here[:, lanes]
            mix_p[block] = mixed[:, lanes]
            adj_p[block] = adjoint[:, lanes]
        return 0

    lax.fori_loop(0, n_parts, turn, 0)

    def wide(ref, block, mode):
        return jnp.broadcast_to(ref[block, pl.ds(mode, 1), :], (SUB, LANES))

    def half_rows(ref, block, half):
        return ref[block, half * SUB:(half + 1) * SUB, :]

    def rows_at(ref, block, step):
        return ref[block, step * SUB:(step + 1) * SUB, :]

    def tree(terms):
        while len(terms) > 1:
            terms = [sum(terms[place:place + 2][1:], terms[place]) for place in range(0, len(terms), 2)]
        return terms[0]

    def cut(array):
        return [array[step * SUB:(step + 1) * SUB] for step in range(steps)]

    def states_of(block, inner):
        for half in range(halves):
            lams = [wide(lam_row, block, half * SUB + mode) for mode in range(SUB)]
            lasts = [rows_at(mix_p, block, 0)] * SUB
            firsts = [rows_at(adj_p, block, steps - 1)] * SUB
            for step in range(1, steps):
                mix, adj = rows_at(mix_p, block, step), rows_at(adj_p, block, steps - 1 - step)
                lasts = [have * lam + mix for have, lam in zip(lasts, lams)]
                firsts = [have * lam + adj for have, lam in zip(firsts, lams)]
            for mode in range(SUB):
                up_turn[inner, half, mode] = lasts[mode]
                down_turn[inner, half, mode] = firsts[mode]
        for half in range(halves):
            tile = block * halves + half
            lam16 = half_rows(lam16_row, block, half)
            lasts = [up_turn[inner, half, :, chunk, :] for chunk in range(SUB)]
            firsts = [down_turn[inner, half, :, chunk, :] for chunk in range(SUB)]
            state = lasts[0]
            lag = jnp.zeros_like(state)
            for chunk in range(1, SUB):
                before[tile, chunk] = state
                lag = lag + firsts[chunk] * state
                state = state * lam16 + lasts[chunk]
            state_out[tile, 0] = state
            lag_out[tile] = lag
            state = firsts[-1]
            for chunk in range(SUB - 2, -1, -1):
                after[tile, chunk] = state
                state = state * lam16 + firsts[chunk]
            state_out[tile, 1] = state

    def first_pass(index, _):
        piece = lax.rem(owner_pieces * (my_local + 1) + index, n_pieces)
        for inner in range(piece_blocks):
            states_of(piece * piece_blocks + inner, inner)

        @pl.when(index == 0)
        def _():
            pl.semaphore_wait(barrier, n_ctx - 1 + n_seq - 1)

        owner, place = piece // owner_pieces, lax.rem(piece, owner_pieces)

        @pl.when(owner != my_local)
        def _():
            state_copy(owner, place, my_local).start()

        @pl.when(owner == my_local)
        def _():
            state_in[my_local, pl.ds(place * piece_tiles, piece_tiles)] = state_out[pl.ds(piece * piece_tiles, piece_tiles)]

        return 0

    lax.fori_loop(0, n_pieces, first_pass, 0)

    def chunk_terms(block):
        mix = cut(mix_p[block])
        adj = cut(adj_p[block])
        lam = [lam_row[block, pl.ds(half * SUB, SUB), :] for half in range(halves)]
        power = [weight_row[block, pl.ds(half * SUB, SUB), :] for half in range(halves)]
        taps = []
        for step in range(steps):
            taps.append(jnp.broadcast_to(jnp.sum(sum(power), axis=0, keepdims=True), (SUB, LANES)))
            power = [left * right for left, right in zip(power, lam)]
        totals = [taps[0] * rows for rows in mix]
        for lag in range(1, steps):
            for step in range(lag, steps):
                totals[step] = totals[step] + taps[lag] * mix[step - lag]
        for step in range(steps):
            conv_p[block, step * SUB:(step + 1) * SUB, :] = totals[step]
        totals = [taps[0] * rows for rows in adj]
        for lag in range(1, steps):
            for step in range(steps - lag):
                totals[step] = totals[step] + taps[lag] * adj[step + lag]
        for step in range(steps):
            back_p[block, step * SUB:(step + 1) * SUB, :] = totals[step]
        totals = [rows * mix[0] for rows in adj]
        for step in range(1, steps):
            for lag in range(steps - step):
                totals[lag] = totals[lag] + adj[step + lag] * mix[step]
        levels = [jnp.broadcast_to(jnp.sum(total, axis=0, keepdims=True), (SUB, LANES)) for total in totals]
        sums = [levels[-1]] * halves
        for level in levels[-2::-1]:
            sums = [have * left + level for have, left in zip(sums, lam)]
        for half in range(halves):
            tile = block * halves + half
            lag_out[tile] = sums[half] + lam[half] * lag_out[tile]

    def second_pass(index, _):
        piece = lax.rem(owner_pieces * (my_local + 1) + index, n_pieces)
        for inner in range(piece_blocks):
            chunk_terms(piece * piece_blocks + inner)
        for inner in range(piece_tiles // per_sum):
            start = piece * piece_tiles + inner * per_sum
            owner = lax.rem(start, per_owner) // per_sum * LOCAL + start // per_owner

            @pl.when(owner != me)
            def _():
                lag_copy(owner, me).start()

            @pl.when(owner == me)
            def _():
                lag_in[me] = lag_out[pl.ds(sum_start(me), per_sum)]

        return 0

    lax.fori_loop(0, n_pieces // 4, second_pass, 0)

    def local_peer(distance):
        return lax.rem(my_local + distance, LOCAL)

    def group_peer(distance):
        return lax.rem(my_group + distance, n_groups)

    for distance in range(1, LOCAL):
        source = local_peer(LOCAL - distance)
        for place in range(owner_pieces):
            state_copy(source, place, source).wait_recv()
    my_first = my_local * per_owner
    for place in range(per_owner):
        hop = jnp.exp(-float(length) * rate_tile[my_first + place])
        carried = state_in[0, place, 0]
        for source in range(1, LOCAL):
            carry_out[source, place, 0] = carried
            carried = carried * hop + state_in[source, place, 0]
        hop_up[place] = carried
        carried = state_in[LOCAL - 1, place, 1]
        for source in range(LOCAL - 2, -1, -1):
            carry_out[source, place, 1] = carried
            carried = carried * hop + state_in[source, place, 1]
        hop_down[place] = carried
    for distance in range(1, n_groups):
        target = group_peer(distance)

        @pl.when(target > my_group)
        def _():
            hop_copy(hop_up, target, my_group).start()

        @pl.when(target < my_group)
        def _():
            hop_copy(hop_down, target, my_group).start()

    hop_in[my_group] = jnp.zeros((per_owner, SUB, LANES), F32)

    lax.fori_loop(n_pieces // 4, 3 * n_pieces // 4, second_pass, 0)

    for distance in range(1, n_groups):
        source = group_peer(n_groups - distance)
        hop_copy(hop_up, source, source).wait_recv()
    for place in range(per_owner):
        rate = rate_tile[my_first + place]
        hop = jnp.exp(-float(length) * rate)
        far = jnp.exp(-float(length * LOCAL) * rate)
        carried = jnp.zeros((SUB, LANES), F32)
        for group in range(n_groups):
            carried = jnp.where(group < my_group, carried * far + hop_in[group, place], carried)
        cross = jnp.zeros((SUB, LANES), F32)
        for source in range(LOCAL):
            total = carry_out[source, place, 0] + carried if source else carried
            carry_out[source, place, 0] = total
            cross = cross + total * state_in[source, place, 1]
            carried = carried * hop
        cross_out[place] = jnp.exp(-rate) * cross
        carried = jnp.zeros((SUB, LANES), F32)
        for group in range(n_groups - 1, -1, -1):
            carried = jnp.where(group > my_group, carried * far + hop_in[group, place], carried)
        for source in range(LOCAL - 1, -1, -1):
            carry_out[source, place, 1] = carry_out[source, place, 1] + carried if source < LOCAL - 1 else carried
            carried = carried * hop
    for place in range(owner_pieces):
        for distance in range(1, LOCAL):
            carry_copy(local_peer(distance), place, my_local).start()
    for distance in range(1, n_groups):
        cross_copy(group_peer(distance), my_group).start()
    carry_in[pl.ds(my_first, per_owner)] = carry_out[my_local]
    cross_in[my_group] = cross_out[pl.ds(my_group * per_sum, per_sum)]

    lax.fori_loop(3 * n_pieces // 4, n_pieces, second_pass, 0)

    def finish(block, inner):
        cols = columns_of(block)
        for half in range(halves):
            tile = block * halves + half
            lam16 = half_rows(lam16_row, block, half)
            lead = half_rows(lam_row, block, half) * half_rows(weight_row, block, half)
            state = carry_in[tile, 0]
            for chunk in range(SUB):
                up_turn[inner, half, chunk] = lead * (state + before[tile, chunk] if chunk else state)
                state = state * lam16
            state = carry_in[tile, 1]
            for chunk in range(SUB - 1, -1, -1):
                down_turn[inner, half, chunk] = lead * (state + after[tile, chunk] if chunk < SUB - 1 else state)
                state = state * lam16
        lams = [wide(lam_row, block, mode) for mode in range(modes)]

        def put(place, step, factor, pair):
            rows = pl.ds(step * SUB, 2 * SUB)
            target = (out, grad_query, grad_key, grad_value)[place]
            target[rows, cols] = (factor[block, rows, :] * pair).astype(jnp.bfloat16)

        terms = [up_turn[inner, mode // SUB, :, mode % SUB, :] for mode in range(modes)]
        sums = []
        for step in range(steps):
            sums.append(rows_at(conv_p, block, step) + tree(terms))
            terms = [term * lam for term, lam in zip(terms, lams)]
            if step % 2:
                pair = jnp.concatenate(sums, axis=0)
                put(0, step - 1, query_p, pair)
                put(1, step - 1, cot_p, pair)
                sums = []
        terms = [down_turn[inner, mode // SUB, :, mode % SUB, :] for mode in range(modes)]
        for step in range(steps - 1, -1, -1):
            sums.insert(0, rows_at(back_p, block, step) + tree(terms))
            terms = [term * lam for term, lam in zip(terms, lams)]
            if step % 2 == 0:
                pair = jnp.concatenate(sums, axis=0)
                put(2, step, value_p, pair)
                put(3, step, key_p, pair)
                sums = []

    own_copy = pltpu.make_async_copy(grad_own, summed(grad_all, me), own_sem)

    def last_pass(index, _):
        owner = lax.rem(my_local + LOCAL - index // owner_pieces, LOCAL)
        place = lax.rem(index, owner_pieces)

        @pl.when(owner != my_local)
        def _():
            carry_copy(owner, place, owner).wait_recv()

        for inner in range(piece_blocks):
            finish((owner * owner_pieces + place) * piece_blocks + inner, inner)

        @pl.when(index == n_pieces // 4)
        def _():
            for distance in range(1, n_ctx):
                source = peer(n_ctx - distance)
                lag_copy(source, source).wait_recv()
            for distance in range(1, n_groups):
                source = group_peer(n_groups - distance)
                cross_copy(source, source).wait_recv()
            for place in range(per_sum):
                total = lag_in[0, place]
                for source in range(1, n_ctx):
                    total = total + lag_in[source, place]
                for source in range(n_groups):
                    total = total + cross_in[source, place]
                part_in[my_seq, place] = total * scale_tile[sum_start(me) + place]
            for distance in range(1, n_seq):
                part_copy(seq_peer(distance), my_seq).start()

        @pl.when(index == 5 * n_pieces // 8)
        def _():
            for distance in range(1, n_seq):
                source = seq_peer(n_seq - distance)
                part_copy(source, source).wait_recv()
            for place in range(per_sum):
                total = part_in[0, place]
                for source in range(1, n_seq):
                    total = total + part_in[source, place]
                grad_own[place] = total * (1.0 / (length * n_ctx * n_seq))
            for distance in range(1, n_ctx):
                grad_copy(peer(distance), me).start()
            own_copy.start()

        return 0

    lax.fori_loop(0, n_pieces, last_pass, 0)

    for distance in range(1, n_ctx):
        source = peer(n_ctx - distance)
        grad_copy(source, source).wait_recv()
    own_copy.wait()
    for distance in range(1, n_ctx):
        target = peer(distance)
        lag_copy(target, me).wait_send()
        grad_copy(target, me).wait_send()
    for distance in range(1, LOCAL):
        target = local_peer(distance)
        for place in range(owner_pieces):
            state_copy(target, place, my_local).wait_send()
            carry_copy(target, place, my_local).wait_send()
    for distance in range(1, n_groups):
        target = group_peer(distance)
        hop_copy(hop_up, target, my_group).wait_send()
        cross_copy(target, my_group).wait_send()
    for distance in range(1, n_seq):
        part_copy(seq_peer(distance), my_seq).wait_send()


def writer(
    out_p, grad_query_p, grad_key_p, grad_value_p, grad_tiles, out, grad_query, grad_key, grad_value, grad_res,
    turned, grad_rows, store_sem, grad_sem,
):
    length, channels = out.shape
    n_parts = store_sem.shape[1]
    part = channels // n_parts
    halves = grad_res.shape[0] // SUB
    sources = (out_p, grad_query_p, grad_key_p, grad_value_p)
    targets = (out, grad_query, grad_key, grad_value)
    for tile in range(grad_tiles.shape[0]):
        block, half = divmod(tile, halves)
        grad_rows[half * SUB:(half + 1) * SUB, block * LANES:(block + 1) * LANES] = grad_tiles[tile]
    stores = [pltpu.make_async_copy(grad_rows, grad_res, grad_sem)]
    stores[-1].start()
    to_tokens = step_order(length, length // SUB, True)
    for place in range(n_parts):
        cols = slice(place * part, (place + 1) * part)
        for index in range(4):
            where = (slice(index * length, (index + 1) * length), cols)
            turned[where] = jnp.dot(to_tokens, sources[index][:, cols], preferred_element_type=F32).astype(jnp.bfloat16)
            stores.append(pltpu.make_async_copy(turned.at[where], targets[index].at[:, cols], store_sem.at[index, place]))
            stores[-1].start()
    for copy in stores:
        copy.wait()


def on_device(n_ctx, n_seq, query_input, key_input, value_input, cotangent, residues, decay_rates):
    _, length, channels = query_input.shape
    modes = residues.shape[1]
    n_blocks = channels // LANES
    halves = modes // SUB
    n_tiles = n_blocks * halves
    n_groups = n_ctx // LOCAL
    per_owner = n_tiles // LOCAL
    per_sum = per_owner // n_groups
    piece_blocks = max(1, per_owner // halves // 2)
    owner_pieces = per_owner // halves // piece_blocks

    def rows():
        return pltpu.VMEM((n_blocks, length, LANES), F32)

    def tiles(*leading):
        return pltpu.VMEM(leading + (SUB, LANES), F32)

    signal = jax.ShapeDtypeStruct((length, channels), jnp.bfloat16)
    hbm = pl.BlockSpec(memory_space=pltpu.HBM)
    vmem = pl.BlockSpec(memory_space=pltpu.VMEM)
    n_parts = 4
    wide_rows = [pltpu.VMEM((length, channels), jnp.bfloat16) for _ in range(4)]
    results = pl.pallas_call(
        functools.partial(kernel, n_ctx, n_seq, n_parts),
        out_shape=[signal] * 4 + [jax.ShapeDtypeStruct((n_tiles, SUB, LANES), F32)],
        in_specs=[hbm] * 4 + [vmem],
        out_specs=[vmem] * 5,
        scratch_shapes=wide_rows
        + [rows() for _ in range(8)]
        + [tiles(n_tiles, SUB), tiles(n_tiles, SUB)]
        + [tiles(piece_blocks, halves, SUB) for _ in range(2)]
        + [pltpu.VMEM((n_blocks, modes, LANES), F32) for _ in range(3)]
        + [tiles(n_tiles), tiles(n_tiles)]
        + [
            tiles(n_tiles, 2), tiles(LOCAL, per_owner, 2), tiles(LOCAL, per_owner, 2), tiles(n_tiles, 2),
            tiles(per_owner), tiles(per_owner), tiles(n_groups, per_owner),
            tiles(per_owner), tiles(n_groups, per_sum), tiles(n_tiles), tiles(n_ctx, per_sum),
            tiles(n_seq, per_sum), tiles(per_sum),
        ]
        + [pltpu.SemaphoreType.DMA((LOCAL, owner_pieces)) for _ in range(4)]
        + [pltpu.SemaphoreType.DMA((n_groups,)) for _ in range(4)]
        + [pltpu.SemaphoreType.DMA((n_ctx,)) for _ in range(4)]
        + [pltpu.SemaphoreType.DMA((n_seq,)) for _ in range(2)]
        + [pltpu.SemaphoreType.DMA((4, n_parts)), pltpu.SemaphoreType.DMA],
        compiler_params=pltpu.CompilerParams(
            collective_id=0, has_side_effects=True, vmem_limit_bytes=820 * 64 * 1024
        ),
        cost_estimate=pl.CostEstimate(flops=100_000_000, bytes_accessed=4_500_000, transcendentals=1_000_000),
        name="modal_states",
    )(query_input[0], key_input[0], value_input[0], cotangent[0], jnp.concatenate([decay_rates.T, residues.T], axis=0))
    results = pl.pallas_call(
        writer,
        out_shape=[signal] * 4 + [jax.ShapeDtypeStruct((modes, channels), F32)],
        in_specs=[vmem] * 5,
        out_specs=[hbm] * 5,
        scratch_shapes=[
            pltpu.VMEM((4 * length, channels), jnp.bfloat16), pltpu.VMEM((modes, channels), F32),
            pltpu.SemaphoreType.DMA((4, n_parts)), pltpu.SemaphoreType.DMA,
        ],
        compiler_params=pltpu.CompilerParams(vmem_limit_bytes=16 * 1024 * 1024),
        cost_estimate=pl.CostEstimate(flops=300_000_000, bytes_accessed=4_500_000, transcendentals=0),
        name="token_order",
    )(*results)
    return tuple(array[None] for array in results[:4]) + (results[4].T,)


def solution(mesh):
    wide = P("seq", "ctx", None)
    return jax.shard_map(
        functools.partial(on_device, mesh.shape["ctx"], mesh.shape["seq"]),
        mesh=mesh,
        in_specs=(wide, wide, wide, wide, P(), P()),
        out_specs=(wide, wide, wide, wide, P()),
        check_vma=False,
    )
```

```python
import functools

import jax
import jax.numpy as jnp
from jax import lax
from jax.experimental import pallas as pl
from jax.experimental.pallas import tpu as pltpu
from jax.sharding import PartitionSpec as P

SUB = 8
LANES = 128
LOCAL = 4
MESH = pl.DeviceIdType.MESH
F32 = jnp.float32


def one_minus_exp(u):
    total = jnp.ones_like(u)
    for order in range(8, 1, -1):
        total = 1.0 - (u / order) * total
    return u * total


def columns_of(block):
    return pl.ds(pl.multiple_of(block * LANES, LANES), LANES)


def step_order(length, steps, inverse):
    row = lax.broadcasted_iota(jnp.int32, (length, length), 0)
    col = lax.broadcasted_iota(jnp.int32, (length, length), 1)
    if inverse:
        row, col = col, row
    return jnp.where(col == steps * (row % SUB) + row // SUB, 1.0, 0.0).astype(jnp.bfloat16)


def kernel(
    n_ctx, n_seq, n_parts, query_hbm, key_hbm, value_hbm, cot_hbm, param_ref,
    out, grad_query, grad_key, grad_value, grad_all,
    query, key, value, cot,
    query_p, key_p, value_p, cot_p, mix_p, adj_p, conv_p, back_p, before, after, up_turn, down_turn,
    lam_row, lam16_row, weight_row, rate_tile, scale_tile,
    state_out, state_in, carry_out, carry_in, hop_up, hop_down, hop_in,
    cross_out, cross_in, lag_out, lag_in, grad_own,
    state_send, state_recv, carry_send, carry_recv, hop_send, hop_recv, cross_send, cross_recv,
    lag_send, lag_recv, grad_send, grad_recv, load_sem, own_sem,
):
    me = lax.axis_index("ctx")
    my_seq = lax.axis_index("seq")
    length, channels = query.shape
    modes = param_ref.shape[0] // 2
    steps = length // SUB
    n_blocks = channels // LANES
    halves = modes // SUB
    n_tiles = n_blocks * halves
    n_groups = n_ctx // LOCAL
    my_group, my_local = me // LOCAL, lax.rem(me, LOCAL)
    per_owner = n_tiles // LOCAL
    per_sum = per_owner // n_groups
    owner_blocks = per_owner // halves
    piece_blocks = max(1, owner_blocks // 2)
    owner_pieces = owner_blocks // piece_blocks
    piece_tiles = piece_blocks * halves
    n_pieces = n_blocks // piece_blocks
    part = channels // n_parts

    def load(index, place):
        cols = pl.ds(pl.multiple_of(place * part, LANES), part)
        source = (key_hbm, value_hbm, query_hbm, cot_hbm)[index]
        target = (key, value, query, cot)[index]
        return pltpu.make_async_copy(source.at[:, cols], target.at[:, cols], load_sem.at[index, place])

    for place in range(n_parts):
        for index in range(4):
            load(index, place).start()

    def peer(distance):
        return lax.rem(me + distance, n_ctx)

    def seq_peer(distance):
        return lax.rem(my_seq + distance, n_seq)

    def remote(src, dst, send, recv, target):
        return pltpu.make_async_remote_copy(
            src_ref=src, dst_ref=dst, send_sem=send, recv_sem=recv,
            device_id=target, device_id_type=MESH,
        )

    def piece_of(ref, piece):
        return ref.at[pl.ds(piece * piece_tiles, piece_tiles)]

    def sum_start(owner):
        return lax.rem(owner, LOCAL) * per_owner + owner // LOCAL * per_sum

    def summed(ref, owner):
        return ref.at[pl.ds(sum_start(owner), per_sum)]

    def state_copy(owner, place, slot):
        return remote(
            piece_of(state_out, owner * owner_pieces + place), piece_of(state_in.at[slot], place),
            state_send.at[owner, place], state_recv.at[slot, place], {"ctx": my_group * LOCAL + owner},
        )

    def carry_copy(target, place, slot):
        return remote(
            piece_of(carry_out.at[target], place), piece_of(carry_in, slot * owner_pieces + place),
            carry_send.at[target, place], carry_recv.at[slot, place], {"ctx": my_group * LOCAL + target},
        )

    def hop_copy(source, target, slot):
        return remote(source, hop_in.at[slot], hop_send.at[target], hop_recv.at[slot], {"ctx": target * LOCAL + my_local})

    def cross_copy(target, target_seq, slot):
        return remote(
            cross_out.at[pl.ds(target * per_sum, per_sum)], cross_in.at[slot],
            cross_send.at[target * n_seq + target_seq], cross_recv.at[slot],
            {"ctx": target * LOCAL + my_local, "seq": target_seq},
        )

    def lag_copy(owner, slot):
        return remote(summed(lag_out, owner), lag_in.at[slot], lag_send.at[owner], lag_recv.at[slot], {"ctx": owner})

    def grad_copy(target, slot):
        return remote(grad_own, summed(grad_all, slot), grad_send.at[target], grad_recv.at[slot], {"ctx": target})

    barrier = pltpu.get_barrier_semaphore()
    for distance in range(1, n_ctx):
        pl.semaphore_signal(barrier, inc=1, device_id={"ctx": peer(distance)}, device_id_type=MESH)
    for distance in range(1, n_seq):
        for group in range(n_groups):
            target = {"ctx": lax.rem(my_group + group, n_groups) * LOCAL + my_local, "seq": seq_peer(distance)}
            pl.semaphore_signal(barrier, inc=1, device_id=target, device_id_type=MESH)

    for block in range(n_blocks):
        cols = slice(block * LANES, (block + 1) * LANES)
        rate = param_ref[:modes, cols]
        scale = jnp.sqrt(one_minus_exp(2.0 * rate))
        lam_row[block] = jnp.exp(-rate)
        lam16_row[block] = jnp.exp(-float(steps) * rate)
        weight_row[block] = param_ref[modes:, cols] * scale
        for half in range(halves):
            rows = slice(half * SUB, (half + 1) * SUB)
            rate_tile[block * halves + half] = rate[rows]
            scale_tile[block * halves + half] = scale[rows]

    to_steps = step_order(length, steps, False)

    def turn(place, _):
        cols = pl.ds(pl.multiple_of(place * part, LANES), part)
        for index in range(4):
            load(index, place).wait()
        key_here, value_here, query_here, cot_here = [
            jnp.dot(to_steps, ref[:, cols], preferred_element_type=F32) for ref in (key, value, query, cot)
        ]
        mixed = key_here * value_here
        adjoint = cot_here * query_here
        for inner in range(part // LANES):
            block = place * (part // LANES) + inner
            lanes = slice(inner * LANES, (inner + 1) * LANES)
            query_p[block] = query_here[:, lanes]
            key_p[block] = key_here[:, lanes]
            value_p[block] = value_here[:, lanes]
            cot_p[block] = cot_here[:, lanes]
            mix_p[block] = mixed[:, lanes]
            adj_p[block] = adjoint[:, lanes]
        return 0

    lax.fori_loop(0, n_parts, turn, 0)

    def wide(ref, block, mode):
        return jnp.broadcast_to(ref[block, pl.ds(mode, 1), :], (SUB, LANES))

    def half_rows(ref, block, half):
        return ref[block, half * SUB:(half + 1) * SUB, :]

    def rows_at(ref, block, step):
        return ref[block, step * SUB:(step + 1) * SUB, :]

    def tree(terms):
        while len(terms) > 1:
            terms = [sum(terms[place:place + 2][1:], terms[place]) for place in range(0, len(terms), 2)]
        return terms[0]

    def cut(array):
        return [array[step * SUB:(step + 1) * SUB] for step in range(steps)]

    def states_of(block, inner):
        for half in range(halves):
            lams = [wide(lam_row, block, half * SUB + mode) for mode in range(SUB)]
            lasts = [rows_at(mix_p, block, 0)] * SUB
            firsts = [rows_at(adj_p, block, steps - 1)] * SUB
            for step in range(1, steps):
                mix, adj = rows_at(mix_p, block, step), rows_at(adj_p, block, steps - 1 - step)
                lasts = [have * lam + mix for have, lam in zip(lasts, lams)]
                firsts = [have * lam + adj for have, lam in zip(firsts, lams)]
            for mode in range(SUB):
                up_turn[inner, half, mode] = lasts[mode]
                down_turn[inner, half, mode] = firsts[mode]
        for half in range(halves):
            tile = block * halves + half
            lam16 = half_rows(lam16_row, block, half)
            lasts = [up_turn[inner, half, :, chunk, :] for chunk in range(SUB)]
            firsts = [down_turn[inner, half, :, chunk, :] for chunk in range(SUB)]
            state = lasts[0]
            lag = jnp.zeros_like(state)
            for chunk in range(1, SUB):
                before[tile, chunk] = state
                lag = lag + firsts[chunk] * state
                state = state * lam16 + lasts[chunk]
            state_out[tile, 0] = state
            lag_out[tile] = lag
            state = firsts[-1]
            for chunk in range(SUB - 2, -1, -1):
                after[tile, chunk] = state
                state = state * lam16 + firsts[chunk]
            state_out[tile, 1] = state

    def first_pass(index, _):
        piece = lax.rem(owner_pieces * (my_local + 1) + index, n_pieces)
        for inner in range(piece_blocks):
            states_of(piece * piece_blocks + inner, inner)

        @pl.when(index == 0)
        def _():
            pl.semaphore_wait(barrier, n_ctx - 1 + (n_seq - 1) * n_groups)

        owner, place = piece // owner_pieces, lax.rem(piece, owner_pieces)

        @pl.when(owner != my_local)
        def _():
            state_copy(owner, place, my_local).start()

        @pl.when(owner == my_local)
        def _():
            state_in[my_local, pl.ds(place * piece_tiles, piece_tiles)] = state_out[pl.ds(piece * piece_tiles, piece_tiles)]

        return 0

    lax.fori_loop(0, n_pieces, first_pass, 0)

    def lag_terms(block):
        mix = cut(mix_p[block])
        adj = cut(adj_p[block])
        lam = [lam_row[block, pl.ds(half * SUB, SUB), :] for half in range(halves)]
        totals = [rows * mix[0] for rows in adj]
        for step in range(1, steps):
            for lag in range(steps - step):
                totals[lag] = totals[lag] + adj[step + lag] * mix[step]
        levels = [jnp.broadcast_to(jnp.sum(total, axis=0, keepdims=True), (SUB, LANES)) for total in totals]
        sums = [levels[-1]] * halves
        for level in levels[-2::-1]:
            sums = [have * left + level for have, left in zip(sums, lam)]
        for half in range(halves):
            tile = block * halves + half
            lag_out[tile] = sums[half] + lam[half] * lag_out[tile]

    def chunk_terms(block):
        mix = cut(mix_p[block])
        adj = cut(adj_p[block])
        lam = [lam_row[block, pl.ds(half * SUB, SUB), :] for half in range(halves)]
        power = [weight_row[block, pl.ds(half * SUB, SUB), :] for half in range(halves)]
        taps = []
        for step in range(steps):
            taps.append(jnp.broadcast_to(jnp.sum(sum(power), axis=0, keepdims=True), (SUB, LANES)))
            power = [left * right for left, right in zip(power, lam)]
        totals = [taps[0] * rows for rows in mix]
        for lag in range(1, steps):
            for step in range(lag, steps):
                totals[step] = totals[step] + taps[lag] * mix[step - lag]
        for step in range(steps):
            conv_p[block, step * SUB:(step + 1) * SUB, :] = totals[step]
        totals = [taps[0] * rows for rows in adj]
        for lag in range(1, steps):
            for step in range(steps - lag):
                totals[step] = totals[step] + taps[lag] * adj[step + lag]
        for step in range(steps):
            back_p[block, step * SUB:(step + 1) * SUB, :] = totals[step]
    def lag_pass(index, _):
        piece = lax.rem(owner_pieces * (my_local + 1) + index, n_pieces)
        for inner in range(piece_blocks):
            lag_terms(piece * piece_blocks + inner)
        for inner in range(piece_tiles // per_sum):
            start = piece * piece_tiles + inner * per_sum
            owner = lax.rem(start, per_owner) // per_sum * LOCAL + start // per_owner

            @pl.when(owner != me)
            def _():
                lag_copy(owner, me).start()

            @pl.when(owner == me)
            def _():
                lag_in[me] = lag_out[pl.ds(sum_start(me), per_sum)]

        return 0

    lax.fori_loop(0, n_pieces, lag_pass, 0)

    def second_pass(piece, _):
        for inner in range(piece_blocks):
            chunk_terms(piece * piece_blocks + inner)
        return 0

    def local_peer(distance):
        return lax.rem(my_local + distance, LOCAL)

    def group_peer(distance):
        return lax.rem(my_group + distance, n_groups)

    for distance in range(1, LOCAL):
        source = local_peer(LOCAL - distance)
        for place in range(owner_pieces):
            state_copy(source, place, source).wait_recv()
    my_first = my_local * per_owner
    for place in range(per_owner):
        hop = jnp.exp(-float(length) * rate_tile[my_first + place])
        carried = state_in[0, place, 0]
        for source in range(1, LOCAL):
            carry_out[source, place, 0] = carried
            carried = carried * hop + state_in[source, place, 0]
        hop_up[place] = carried
        carried = state_in[LOCAL - 1, place, 1]
        for source in range(LOCAL - 2, -1, -1):
            carry_out[source, place, 1] = carried
            carried = carried * hop + state_in[source, place, 1]
        hop_down[place] = carried
    for distance in range(1, n_groups):
        target = group_peer(distance)

        @pl.when(target > my_group)
        def _():
            hop_copy(hop_up, target, my_group).start()

        @pl.when(target < my_group)
        def _():
            hop_copy(hop_down, target, my_group).start()

    hop_in[my_group] = jnp.zeros((per_owner, SUB, LANES), F32)

    lax.fori_loop(0, 5 * n_pieces // 8, second_pass, 0)

    for distance in range(1, n_groups):
        source = group_peer(n_groups - distance)
        hop_copy(hop_up, source, source).wait_recv()
    for place in range(per_owner):
        rate = rate_tile[my_first + place]
        hop = jnp.exp(-float(length) * rate)
        far = jnp.exp(-float(length * LOCAL) * rate)
        carried = jnp.zeros((SUB, LANES), F32)
        for group in range(n_groups):
            carried = jnp.where(group < my_group, carried * far + hop_in[group, place], carried)
        cross = jnp.zeros((SUB, LANES), F32)
        for source in range(LOCAL):
            total = carry_out[source, place, 0] + carried if source else carried
            carry_out[source, place, 0] = total
            cross = cross + total * state_in[source, place, 1]
            carried = carried * hop
        cross_out[place] = jnp.exp(-rate) * cross
        carried = jnp.zeros((SUB, LANES), F32)
        for group in range(n_groups - 1, -1, -1):
            carried = jnp.where(group > my_group, carried * far + hop_in[group, place], carried)
        for source in range(LOCAL - 1, -1, -1):
            carry_out[source, place, 1] = carry_out[source, place, 1] + carried if source < LOCAL - 1 else carried
            carried = carried * hop
    for place in range(owner_pieces):
        for distance in range(1, LOCAL):
            carry_copy(local_peer(distance), place, my_local).start()
    carry_in[pl.ds(my_first, per_owner)] = carry_out[my_local]

    for distance in range(1, n_ctx):
        source = peer(n_ctx - distance)
        lag_copy(source, source).wait_recv()
    for place in range(per_sum):
        total = cross_out[my_group * per_sum + place]
        for source in range(n_ctx):
            total = total + lag_in[source, place]
        cross_out[my_group * per_sum + place] = total
    counterparts = [(group, seq) for group in range(n_groups) for seq in range(n_seq)][1:]
    my_slot = my_group * n_seq + my_seq
    for group, seq in counterparts:
        cross_copy(group_peer(group), seq_peer(seq), my_slot).start()
    cross_in[my_slot] = cross_out[pl.ds(my_group * per_sum, per_sum)]

    lax.fori_loop(5 * n_pieces // 8, n_pieces, second_pass, 0)

    def finish(block, inner):
        cols = columns_of(block)
        for half in range(halves):
            tile = block * halves + half
            lam16 = half_rows(lam16_row, block, half)
            lead = half_rows(lam_row, block, half) * half_rows(weight_row, block, half)
            state = carry_in[tile, 0]
            for chunk in range(SUB):
                up_turn[inner, half, chunk] = lead * (state + before[tile, chunk] if chunk else state)
                state = state * lam16
            state = carry_in[tile, 1]
            for chunk in range(SUB - 1, -1, -1):
                down_turn[inner, half, chunk] = lead * (state + after[tile, chunk] if chunk < SUB - 1 else state)
                state = state * lam16
        lams = [wide(lam_row, block, mode) for mode in range(modes)]

        def put(place, step, factor, pair):
            rows = pl.ds(step * SUB, 2 * SUB)
            target = (out, grad_query, grad_key, grad_value)[place]
            target[rows, cols] = (factor[block, rows, :] * pair).astype(jnp.bfloat16)

        terms = [up_turn[inner, mode // SUB, :, mode % SUB, :] for mode in range(modes)]
        sums = []
        for step in range(steps):
            sums.append(rows_at(conv_p, block, step) + tree(terms))
            terms = [term * lam for term, lam in zip(terms, lams)]
            if step % 2:
                pair = jnp.concatenate(sums, axis=0)
                put(0, step - 1, query_p, pair)
                put(1, step - 1, cot_p, pair)
                sums = []
        terms = [down_turn[inner, mode // SUB, :, mode % SUB, :] for mode in range(modes)]
        for step in range(steps - 1, -1, -1):
            sums.insert(0, rows_at(back_p, block, step) + tree(terms))
            terms = [term * lam for term, lam in zip(terms, lams)]
            if step % 2 == 0:
                pair = jnp.concatenate(sums, axis=0)
                put(2, step, value_p, pair)
                put(3, step, key_p, pair)
                sums = []

    own_copy = pltpu.make_async_copy(grad_own, summed(grad_all, me), own_sem)

    def last_pass(index, _):
        owner = lax.rem(my_local + LOCAL - index // owner_pieces, LOCAL)
        place = lax.rem(index, owner_pieces)

        @pl.when(owner != my_local)
        def _():
            carry_copy(owner, place, owner).wait_recv()

        for inner in range(piece_blocks):
            finish((owner * owner_pieces + place) * piece_blocks + inner, inner)

        @pl.when(index == n_pieces // 2)
        def _():
            for group, seq in counterparts:
                source, source_seq = group_peer(n_groups - group), seq_peer(n_seq - seq)
                cross_copy(source, source_seq, source * n_seq + source_seq).wait_recv()
            for place in range(per_sum):
                total = cross_in[0, place]
                for source in range(1, n_groups * n_seq):
                    total = total + cross_in[source, place]
                grad_own[place] = total * scale_tile[sum_start(me) + place] * (1.0 / (length * n_ctx * n_seq))
            for distance in range(1, n_ctx):
                grad_copy(peer(distance), me).start()
            own_copy.start()

        return 0

    lax.fori_loop(0, n_pieces, last_pass, 0)

    for distance in range(1, n_ctx):
        source = peer(n_ctx - distance)
        grad_copy(source, source).wait_recv()
    own_copy.wait()
    for distance in range(1, n_ctx):
        target = peer(distance)
        lag_copy(target, me).wait_send()
        grad_copy(target, me).wait_send()
    for distance in range(1, LOCAL):
        target = local_peer(distance)
        for place in range(owner_pieces):
            state_copy(target, place, my_local).wait_send()
            carry_copy(target, place, my_local).wait_send()
    for distance in range(1, n_groups):
        target = group_peer(distance)
        hop_copy(hop_up, target, my_group).wait_send()
    for group, seq in counterparts:
        cross_copy(group_peer(group), seq_peer(seq), my_slot).wait_send()


def writer(
    out_p, grad_query_p, grad_key_p, grad_value_p, grad_tiles, out, grad_query, grad_key, grad_value, grad_res,
    turned, grad_rows, store_sem, grad_sem,
):
    length, channels = out.shape
    n_parts = store_sem.shape[1]
    part = channels // n_parts
    halves = grad_res.shape[0] // SUB
    sources = (out_p, grad_query_p, grad_key_p, grad_value_p)
    targets = (out, grad_query, grad_key, grad_value)
    for tile in range(grad_tiles.shape[0]):
        block, half = divmod(tile, halves)
        grad_rows[half * SUB:(half + 1) * SUB, block * LANES:(block + 1) * LANES] = grad_tiles[tile]
    stores = [pltpu.make_async_copy(grad_rows, grad_res, grad_sem)]
    stores[-1].start()
    to_tokens = step_order(length, length // SUB, True)
    for place in range(n_parts):
        cols = slice(place * part, (place + 1) * part)
        for index in range(4):
            where = (slice(index * length, (index + 1) * length), cols)
            turned[where] = jnp.dot(to_tokens, sources[index][:, cols], preferred_element_type=F32).astype(jnp.bfloat16)
            stores.append(pltpu.make_async_copy(turned.at[where], targets[index].at[:, cols], store_sem.at[index, place]))
            stores[-1].start()
    for copy in stores:
        copy.wait()


def on_device(n_ctx, n_seq, query_input, key_input, value_input, cotangent, residues, decay_rates):
    _, length, channels = query_input.shape
    modes = residues.shape[1]
    n_blocks = channels // LANES
    halves = modes // SUB
    n_tiles = n_blocks * halves
    n_groups = n_ctx // LOCAL
    per_owner = n_tiles // LOCAL
    per_sum = per_owner // n_groups
    piece_blocks = max(1, per_owner // halves // 2)
    owner_pieces = per_owner // halves // piece_blocks

    def rows():
        return pltpu.VMEM((n_blocks, length, LANES), F32)

    def tiles(*leading):
        return pltpu.VMEM(leading + (SUB, LANES), F32)

    signal = jax.ShapeDtypeStruct((length, channels), jnp.bfloat16)
    hbm = pl.BlockSpec(memory_space=pltpu.HBM)
    vmem = pl.BlockSpec(memory_space=pltpu.VMEM)
    n_parts = 4
    wide_rows = [pltpu.VMEM((length, channels), jnp.bfloat16) for _ in range(4)]
    results = pl.pallas_call(
        functools.partial(kernel, n_ctx, n_seq, n_parts),
        out_shape=[signal] * 4 + [jax.ShapeDtypeStruct((n_tiles, SUB, LANES), F32)],
        in_specs=[hbm] * 4 + [vmem],
        out_specs=[vmem] * 5,
        scratch_shapes=wide_rows
        + [rows() for _ in range(8)]
        + [tiles(n_tiles, SUB), tiles(n_tiles, SUB)]
        + [tiles(piece_blocks, halves, SUB) for _ in range(2)]
        + [pltpu.VMEM((n_blocks, modes, LANES), F32) for _ in range(3)]
        + [tiles(n_tiles), tiles(n_tiles)]
        + [
            tiles(n_tiles, 2), tiles(LOCAL, per_owner, 2), tiles(LOCAL, per_owner, 2), tiles(n_tiles, 2),
            tiles(per_owner), tiles(per_owner), tiles(n_groups, per_owner),
            tiles(per_owner), tiles(n_groups * n_seq, per_sum), tiles(n_tiles), tiles(n_ctx, per_sum), tiles(per_sum),
        ]
        + [pltpu.SemaphoreType.DMA((LOCAL, owner_pieces)) for _ in range(4)]
        + [pltpu.SemaphoreType.DMA((n_groups,)) for _ in range(2)]
        + [pltpu.SemaphoreType.DMA((n_groups * n_seq,)) for _ in range(2)]
        + [pltpu.SemaphoreType.DMA((n_ctx,)) for _ in range(4)]
        + [pltpu.SemaphoreType.DMA((4, n_parts)), pltpu.SemaphoreType.DMA],
        compiler_params=pltpu.CompilerParams(
            collective_id=0, has_side_effects=True, vmem_limit_bytes=820 * 64 * 1024
        ),
        cost_estimate=pl.CostEstimate(flops=100_000_000, bytes_accessed=4_500_000, transcendentals=1_000_000),
        name="modal_states",
    )(query_input[0], key_input[0], value_input[0], cotangent[0], jnp.concatenate([decay_rates.T, residues.T], axis=0))
    results = pl.pallas_call(
        writer,
        out_shape=[signal] * 4 + [jax.ShapeDtypeStruct((modes, channels), F32)],
        in_specs=[vmem] * 5,
        out_specs=[hbm] * 5,
        scratch_shapes=[
            pltpu.VMEM((4 * length, channels), jnp.bfloat16), pltpu.VMEM((modes, channels), F32),
            pltpu.SemaphoreType.DMA((4, n_parts)), pltpu.SemaphoreType.DMA,
        ],
        compiler_params=pltpu.CompilerParams(vmem_limit_bytes=16 * 1024 * 1024),
        cost_estimate=pl.CostEstimate(flops=300_000_000, bytes_accessed=4_500_000, transcendentals=0),
        name="token_order",
    )(*results)
    return tuple(array[None] for array in results[:4]) + (results[4].T,)


def solution(mesh):
    wide = P("seq", "ctx", None)
    return jax.shard_map(
        functools.partial(on_device, mesh.shape["ctx"], mesh.shape["seq"]),
        mesh=mesh,
        in_specs=(wide, wide, wide, wide, P(), P()),
        out_specs=(wide, wide, wide, wide, P()),
        check_vma=False,
    )
```

```python
import functools

import jax
import jax.numpy as jnp
from jax import lax
from jax.experimental import pallas as pl
from jax.experimental.pallas import tpu as pltpu
from jax.sharding import PartitionSpec as P

SUB = 8
LANES = 128
LOCAL = 4
MESH = pl.DeviceIdType.MESH
F32 = jnp.float32


def one_minus_exp(u):
    total = jnp.ones_like(u)
    for order in range(8, 1, -1):
        total = 1.0 - (u / order) * total
    return u * total


def columns_of(block):
    return pl.ds(pl.multiple_of(block * LANES, LANES), LANES)


def step_order(length, steps, inverse):
    row = lax.broadcasted_iota(jnp.int32, (length, length), 0)
    col = lax.broadcasted_iota(jnp.int32, (length, length), 1)
    if inverse:
        row, col = col, row
    return jnp.where(col == steps * (row % SUB) + row // SUB, 1.0, 0.0).astype(jnp.bfloat16)


def kernel(
    n_ctx, n_seq, n_parts, query_hbm, key_hbm, value_hbm, cot_hbm, param_ref,
    out, grad_query, grad_key, grad_value, grad_all,
    query, key, value, cot,
    query_p, key_p, value_p, cot_p, mix_p, adj_p, conv_p, back_p, before, after, up_turn, down_turn, mix_even, adj_even, mix_odd, adj_odd,
    lam_row, lam16_row, weight_row, rate_tile, scale_tile,
    state_out, state_in, carry_out, carry_in, hop_up, hop_down, hop_in,
    cross_out, cross_in, lag_out, lag_in, grad_own,
    state_send, state_recv, carry_send, carry_recv, hop_send, hop_recv, cross_send, cross_recv,
    lag_send, lag_recv, grad_send, grad_recv, load_sem, own_sem,
):
    me = lax.axis_index("ctx")
    my_seq = lax.axis_index("seq")
    length, channels = query.shape
    modes = param_ref.shape[0] // 2
    steps = length // SUB
    n_blocks = channels // LANES
    halves = modes // SUB
    n_tiles = n_blocks * halves
    n_groups = n_ctx // LOCAL
    my_group, my_local = me // LOCAL, lax.rem(me, LOCAL)
    per_owner = n_tiles // LOCAL
    per_sum = per_owner // n_groups
    owner_blocks = per_owner // halves
    piece_blocks = max(1, owner_blocks // 2)
    owner_pieces = owner_blocks // piece_blocks
    piece_tiles = piece_blocks * halves
    n_pieces = n_blocks // piece_blocks
    part = channels // n_parts

    def load(index, place):
        cols = pl.ds(pl.multiple_of(place * part, LANES), part)
        source = (key_hbm, value_hbm, query_hbm, cot_hbm)[index]
        target = (key, value, query, cot)[index]
        return pltpu.make_async_copy(source.at[:, cols], target.at[:, cols], load_sem.at[index, place])

    def piece_at(index):
        return lax.rem(owner_pieces * (my_local + 1) + index, n_pieces)

    for order in range(n_pieces):
        for index in range(4):
            load(index, piece_at(order)).start()

    def peer(distance):
        return lax.rem(me + distance, n_ctx)

    def seq_peer(distance):
        return lax.rem(my_seq + distance, n_seq)

    def remote(src, dst, send, recv, target):
        return pltpu.make_async_remote_copy(
            src_ref=src, dst_ref=dst, send_sem=send, recv_sem=recv,
            device_id=target, device_id_type=MESH,
        )

    def piece_of(ref, piece):
        return ref.at[pl.ds(piece * piece_tiles, piece_tiles)]

    def sum_start(owner):
        return lax.rem(owner, LOCAL) * per_owner + owner // LOCAL * per_sum

    def summed(ref, owner):
        return ref.at[pl.ds(sum_start(owner), per_sum)]

    def state_copy(owner, place, slot):
        return remote(
            piece_of(state_out, owner * owner_pieces + place), piece_of(state_in.at[slot], place),
            state_send.at[owner, place], state_recv.at[slot, place], {"ctx": my_group * LOCAL + owner},
        )

    def carry_copy(target, place, slot):
        return remote(
            piece_of(carry_out.at[target], place), piece_of(carry_in, slot * owner_pieces + place),
            carry_send.at[target, place], carry_recv.at[slot, place], {"ctx": my_group * LOCAL + target},
        )

    def hop_copy(source, target, slot):
        return remote(source, hop_in.at[slot], hop_send.at[target], hop_recv.at[slot], {"ctx": target * LOCAL + my_local})

    def cross_copy(target, target_seq, slot):
        return remote(
            cross_out.at[pl.ds(target * per_sum, per_sum)], cross_in.at[slot],
            cross_send.at[target * n_seq + target_seq], cross_recv.at[slot],
            {"ctx": target * LOCAL + my_local, "seq": target_seq},
        )

    def lag_copy(owner, slot):
        return remote(summed(lag_out, owner), lag_in.at[slot], lag_send.at[owner], lag_recv.at[slot], {"ctx": owner})

    def grad_copy(target, slot):
        return remote(grad_own, summed(grad_all, slot), grad_send.at[target], grad_recv.at[slot], {"ctx": target})

    barrier = pltpu.get_barrier_semaphore()
    for distance in range(1, n_ctx):
        pl.semaphore_signal(barrier, inc=1, device_id={"ctx": peer(distance)}, device_id_type=MESH)
    for distance in range(1, n_seq):
        for group in range(n_groups):
            target = {"ctx": lax.rem(my_group + group, n_groups) * LOCAL + my_local, "seq": seq_peer(distance)}
            pl.semaphore_signal(barrier, inc=1, device_id=target, device_id_type=MESH)

    for block in range(n_blocks):
        cols = slice(block * LANES, (block + 1) * LANES)
        rate = param_ref[:modes, cols]
        scale = jnp.sqrt(one_minus_exp(2.0 * rate))
        lam_row[block] = jnp.exp(-rate)
        lam16_row[block] = jnp.exp(-float(steps) * rate)
        weight_row[block] = param_ref[modes:, cols] * scale
        for half in range(halves):
            rows = slice(half * SUB, (half + 1) * SUB)
            rate_tile[block * halves + half] = rate[rows]
            scale_tile[block * halves + half] = scale[rows]

    to_steps = step_order(length, steps, False)

    def take(place):
        for index in range(4):
            load(index, place).wait()

    def turn(place, mix_now, adj_now):
        cols = pl.ds(pl.multiple_of(place * part, LANES), part)
        key_here, value_here, query_here, cot_here = [
            jnp.dot(to_steps, ref[:, cols], preferred_element_type=F32) for ref in (key, value, query, cot)
        ]
        mixed = key_here * value_here
        adjoint = cot_here * query_here
        for inner in range(part // LANES):
            block = place * (part // LANES) + inner
            lanes = slice(inner * LANES, (inner + 1) * LANES)
            query_p[block] = query_here[:, lanes]
            key_p[block] = key_here[:, lanes]
            value_p[block] = value_here[:, lanes]
            cot_p[block] = cot_here[:, lanes]
            mix_p[block] = mixed[:, lanes]
            adj_p[block] = adjoint[:, lanes]
            mix_now[inner] = mixed[:, lanes]
            adj_now[inner] = adjoint[:, lanes]

    def wide(ref, block, mode):
        return jnp.broadcast_to(ref[block, pl.ds(mode, 1), :], (SUB, LANES))

    def half_rows(ref, block, half):
        return ref[block, half * SUB:(half + 1) * SUB, :]

    def rows_at(ref, block, step):
        return ref[block, step * SUB:(step + 1) * SUB, :]

    def tree(terms):
        while len(terms) > 1:
            terms = [sum(terms[place:place + 2][1:], terms[place]) for place in range(0, len(terms), 2)]
        return terms[0]

    def cut(array):
        return [array[step * SUB:(step + 1) * SUB] for step in range(steps)]

    def states_of(block, inner, mix_now, adj_now):
        for half in range(halves):
            lams = [wide(lam_row, block, half * SUB + mode) for mode in range(SUB)]
            lasts = [rows_at(mix_now, inner, 0)] * SUB
            firsts = [rows_at(adj_now, inner, steps - 1)] * SUB
            for step in range(1, steps):
                mix, adj = rows_at(mix_now, inner, step), rows_at(adj_now, inner, steps - 1 - step)
                lasts = [have * lam + mix for have, lam in zip(lasts, lams)]
                firsts = [have * lam + adj for have, lam in zip(firsts, lams)]
            for mode in range(SUB):
                up_turn[inner, half, mode] = lasts[mode]
                down_turn[inner, half, mode] = firsts[mode]
        for half in range(halves):
            tile = block * halves + half
            lam16 = half_rows(lam16_row, block, half)
            lasts = [up_turn[inner, half, :, chunk, :] for chunk in range(SUB)]
            firsts = [down_turn[inner, half, :, chunk, :] for chunk in range(SUB)]
            state = lasts[0]
            lag = jnp.zeros_like(state)
            for chunk in range(1, SUB):
                before[tile, chunk] = state
                lag = lag + firsts[chunk] * state
                state = state * lam16 + lasts[chunk]
            state_out[tile, 0] = state
            lag_out[tile] = lag
            state = firsts[-1]
            for chunk in range(SUB - 2, -1, -1):
                after[tile, chunk] = state
                state = state * lam16 + firsts[chunk]
            state_out[tile, 1] = state

    def send_state(piece):
        owner, place = piece // owner_pieces, lax.rem(piece, owner_pieces)

        @pl.when(owner != my_local)
        def _():
            state_copy(owner, place, my_local).start()

        @pl.when(owner == my_local)
        def _():
            state_in[my_local, pl.ds(place * piece_tiles, piece_tiles)] = state_out[pl.ds(piece * piece_tiles, piece_tiles)]

    even, odd = (mix_even, adj_even), (mix_odd, adj_odd)

    def first_piece(order, now, later, last=False):
        piece = piece_at(order)
        if not last:
            following = piece_at(order + 1)
            take(following)
            turn(following, *later)
        for inner in range(piece_blocks):
            states_of(piece * piece_blocks + inner, inner, *now)

        @pl.when(order == 0)
        def _():
            pl.semaphore_wait(barrier, n_ctx - 1 + (n_seq - 1) * n_groups)

        send_state(piece)

    def first_pass(index, _):
        first_piece(2 * index, even, odd)
        first_piece(2 * index + 1, odd, even)
        return 0

    take(piece_at(0))
    turn(piece_at(0), *even)
    lax.fori_loop(0, n_pieces // 2 - 1, first_pass, 0)
    first_piece(n_pieces - 2, even, odd)
    first_piece(n_pieces - 1, odd, even, last=True)

    def lag_terms(block):
        mix = cut(mix_p[block])
        adj = cut(adj_p[block])
        lam = [lam_row[block, pl.ds(half * SUB, SUB), :] for half in range(halves)]
        totals = [rows * mix[0] for rows in adj]
        for step in range(1, steps):
            for lag in range(steps - step):
                totals[lag] = totals[lag] + adj[step + lag] * mix[step]
        levels = [jnp.broadcast_to(jnp.sum(total, axis=0, keepdims=True), (SUB, LANES)) for total in totals]
        sums = [levels[-1]] * halves
        for level in levels[-2::-1]:
            sums = [have * left + level for have, left in zip(sums, lam)]
        for half in range(halves):
            tile = block * halves + half
            lag_out[tile] = sums[half] + lam[half] * lag_out[tile]

    def chunk_terms(block):
        mix = cut(mix_p[block])
        adj = cut(adj_p[block])
        lam = [lam_row[block, pl.ds(half * SUB, SUB), :] for half in range(halves)]
        power = [weight_row[block, pl.ds(half * SUB, SUB), :] for half in range(halves)]
        taps = []
        for step in range(steps):
            taps.append(jnp.broadcast_to(jnp.sum(sum(power), axis=0, keepdims=True), (SUB, LANES)))
            power = [left * right for left, right in zip(power, lam)]
        totals = [taps[0] * rows for rows in mix]
        for lag in range(1, steps):
            for step in range(lag, steps):
                totals[step] = totals[step] + taps[lag] * mix[step - lag]
        for step in range(steps):
            conv_p[block, step * SUB:(step + 1) * SUB, :] = totals[step]
        totals = [taps[0] * rows for rows in adj]
        for lag in range(1, steps):
            for step in range(steps - lag):
                totals[step] = totals[step] + taps[lag] * adj[step + lag]
        for step in range(steps):
            back_p[block, step * SUB:(step + 1) * SUB, :] = totals[step]
    def lag_pass(index, _):
        piece = piece_at(index)
        for inner in range(piece_blocks):
            lag_terms(piece * piece_blocks + inner)
        for inner in range(piece_tiles // per_sum):
            start = piece * piece_tiles + inner * per_sum
            owner = lax.rem(start, per_owner) // per_sum * LOCAL + start // per_owner

            @pl.when(owner != me)
            def _():
                lag_copy(owner, me).start()

            @pl.when(owner == me)
            def _():
                lag_in[me] = lag_out[pl.ds(sum_start(me), per_sum)]

        return 0

    lax.fori_loop(0, n_pieces, lag_pass, 0)

    def second_pass(piece, _):
        for inner in range(piece_blocks):
            chunk_terms(piece * piece_blocks + inner)
        return 0

    def local_peer(distance):
        return lax.rem(my_local + distance, LOCAL)

    def group_peer(distance):
        return lax.rem(my_group + distance, n_groups)

    for distance in range(1, LOCAL):
        source = local_peer(LOCAL - distance)
        for place in range(owner_pieces):
            state_copy(source, place, source).wait_recv()
    my_first = my_local * per_owner
    for place in range(per_owner):
        hop = jnp.exp(-float(length) * rate_tile[my_first + place])
        carried = state_in[0, place, 0]
        for source in range(1, LOCAL):
            carry_out[source, place, 0] = carried
            carried = carried * hop + state_in[source, place, 0]
        hop_up[place] = carried
        carried = state_in[LOCAL - 1, place, 1]
        for source in range(LOCAL - 2, -1, -1):
            carry_out[source, place, 1] = carried
            carried = carried * hop + state_in[source, place, 1]
        hop_down[place] = carried
    for distance in range(1, n_groups):
        target = group_peer(distance)

        @pl.when(target > my_group)
        def _():
            hop_copy(hop_up, target, my_group).start()

        @pl.when(target < my_group)
        def _():
            hop_copy(hop_down, target, my_group).start()

    hop_in[my_group] = jnp.zeros((per_owner, SUB, LANES), F32)

    lax.fori_loop(0, 5 * n_pieces // 8, second_pass, 0)

    for distance in range(1, n_groups):
        source = group_peer(n_groups - distance)
        hop_copy(hop_up, source, source).wait_recv()
    for place in range(per_owner):
        rate = rate_tile[my_first + place]
        hop = jnp.exp(-float(length) * rate)
        far = jnp.exp(-float(length * LOCAL) * rate)
        carried = jnp.zeros((SUB, LANES), F32)
        for group in range(n_groups):
            carried = jnp.where(group < my_group, carried * far + hop_in[group, place], carried)
        cross = jnp.zeros((SUB, LANES), F32)
        for source in range(LOCAL):
            total = carry_out[source, place, 0] + carried if source else carried
            carry_out[source, place, 0] = total
            cross = cross + total * state_in[source, place, 1]
            carried = carried * hop
        cross_out[place] = jnp.exp(-rate) * cross
        carried = jnp.zeros((SUB, LANES), F32)
        for group in range(n_groups - 1, -1, -1):
            carried = jnp.where(group > my_group, carried * far + hop_in[group, place], carried)
        for source in range(LOCAL - 1, -1, -1):
            carry_out[source, place, 1] = carry_out[source, place, 1] + carried if source < LOCAL - 1 else carried
            carried = carried * hop
    for place in range(owner_pieces):
        for distance in range(1, LOCAL):
            carry_copy(local_peer(distance), place, my_local).start()
    carry_in[pl.ds(my_first, per_owner)] = carry_out[my_local]

    for distance in range(1, n_ctx):
        source = peer(n_ctx - distance)
        lag_copy(source, source).wait_recv()
    for place in range(per_sum):
        total = cross_out[my_group * per_sum + place]
        for source in range(n_ctx):
            total = total + lag_in[source, place]
        cross_out[my_group * per_sum + place] = total
    counterparts = [(group, seq) for group in range(n_groups) for seq in range(n_seq)][1:]
    my_slot = my_group * n_seq + my_seq
    for group, seq in counterparts:
        cross_copy(group_peer(group), seq_peer(seq), my_slot).start()
    cross_in[my_slot] = cross_out[pl.ds(my_group * per_sum, per_sum)]

    lax.fori_loop(5 * n_pieces // 8, n_pieces, second_pass, 0)

    def finish(block, inner):
        cols = columns_of(block)
        for half in range(halves):
            tile = block * halves + half
            lam16 = half_rows(lam16_row, block, half)
            lead = half_rows(lam_row, block, half) * half_rows(weight_row, block, half)
            state = carry_in[tile, 0]
            for chunk in range(SUB):
                up_turn[inner, half, chunk] = lead * (state + before[tile, chunk] if chunk else state)
                state = state * lam16
            state = carry_in[tile, 1]
            for chunk in range(SUB - 1, -1, -1):
                down_turn[inner, half, chunk] = lead * (state + after[tile, chunk] if chunk < SUB - 1 else state)
                state = state * lam16
        lams = [wide(lam_row, block, mode) for mode in range(modes)]

        def put(place, step, factor, pair):
            rows = pl.ds(step * SUB, 2 * SUB)
            target = (out, grad_query, grad_key, grad_value)[place]
            target[rows, cols] = (factor[block, rows, :] * pair).astype(jnp.bfloat16)

        terms = [up_turn[inner, mode // SUB, :, mode % SUB, :] for mode in range(modes)]
        sums = []
        for step in range(steps):
            sums.append(rows_at(conv_p, block, step) + tree(terms))
            terms = [term * lam for term, lam in zip(terms, lams)]
            if step % 2:
                pair = jnp.concatenate(sums, axis=0)
                put(0, step - 1, query_p, pair)
                put(1, step - 1, cot_p, pair)
                sums = []
        terms = [down_turn[inner, mode // SUB, :, mode % SUB, :] for mode in range(modes)]
        for step in range(steps - 1, -1, -1):
            sums.insert(0, rows_at(back_p, block, step) + tree(terms))
            terms = [term * lam for term, lam in zip(terms, lams)]
            if step % 2 == 0:
                pair = jnp.concatenate(sums, axis=0)
                put(2, step, value_p, pair)
                put(3, step, key_p, pair)
                sums = []

    own_copy = pltpu.make_async_copy(grad_own, summed(grad_all, me), own_sem)

    def last_pass(index, _):
        owner = lax.rem(my_local + LOCAL - index // owner_pieces, LOCAL)
        place = lax.rem(index, owner_pieces)

        @pl.when(owner != my_local)
        def _():
            carry_copy(owner, place, owner).wait_recv()

        for inner in range(piece_blocks):
            finish((owner * owner_pieces + place) * piece_blocks + inner, inner)

        @pl.when(index == n_pieces // 4)
        def _():
            for group, seq in counterparts:
                source, source_seq = group_peer(n_groups - group), seq_peer(n_seq - seq)
                cross_copy(source, source_seq, source * n_seq + source_seq).wait_recv()
            for place in range(per_sum):
                total = cross_in[0, place]
                for source in range(1, n_groups * n_seq):
                    total = total + cross_in[source, place]
                grad_own[place] = total * scale_tile[sum_start(me) + place] * (1.0 / (length * n_ctx * n_seq))
            for distance in range(1, n_ctx):
                grad_copy(peer(distance), me).start()
            own_copy.start()

        return 0

    lax.fori_loop(0, n_pieces, last_pass, 0)

    for distance in range(1, n_ctx):
        source = peer(n_ctx - distance)
        grad_copy(source, source).wait_recv()
    own_copy.wait()
    for distance in range(1, n_ctx):
        target = peer(distance)
        lag_copy(target, me).wait_send()
        grad_copy(target, me).wait_send()
    for distance in range(1, LOCAL):
        target = local_peer(distance)
        for place in range(owner_pieces):
            state_copy(target, place, my_local).wait_send()
            carry_copy(target, place, my_local).wait_send()
    for distance in range(1, n_groups):
        target = group_peer(distance)
        hop_copy(hop_up, target, my_group).wait_send()
    for group, seq in counterparts:
        cross_copy(group_peer(group), seq_peer(seq), my_slot).wait_send()


def writer(
    out_p, grad_query_p, grad_key_p, grad_value_p, grad_tiles, out, grad_query, grad_key, grad_value, grad_res,
    turned, grad_rows, store_sem, grad_sem,
):
    length, channels = out.shape
    n_parts = store_sem.shape[1]
    part = channels // n_parts
    halves = grad_res.shape[0] // SUB
    sources = (out_p, grad_query_p, grad_key_p, grad_value_p)
    targets = (out, grad_query, grad_key, grad_value)
    for tile in range(grad_tiles.shape[0]):
        block, half = divmod(tile, halves)
        grad_rows[half * SUB:(half + 1) * SUB, block * LANES:(block + 1) * LANES] = grad_tiles[tile]
    stores = [pltpu.make_async_copy(grad_rows, grad_res, grad_sem)]
    stores[-1].start()
    to_tokens = step_order(length, length // SUB, True)
    for place in range(n_parts):
        cols = slice(place * part, (place + 1) * part)
        for index in range(4):
            where = (slice(index * length, (index + 1) * length), cols)
            turned[where] = jnp.dot(to_tokens, sources[index][:, cols], preferred_element_type=F32).astype(jnp.bfloat16)
            stores.append(pltpu.make_async_copy(turned.at[where], targets[index].at[:, cols], store_sem.at[index, place]))
            stores[-1].start()
    for copy in stores:
        copy.wait()


def on_device(n_ctx, n_seq, query_input, key_input, value_input, cotangent, residues, decay_rates):
    _, length, channels = query_input.shape
    modes = residues.shape[1]
    n_blocks = channels // LANES
    halves = modes // SUB
    n_tiles = n_blocks * halves
    n_groups = n_ctx // LOCAL
    per_owner = n_tiles // LOCAL
    per_sum = per_owner // n_groups
    piece_blocks = max(1, per_owner // halves // 2)
    owner_pieces = per_owner // halves // piece_blocks

    def rows():
        return pltpu.VMEM((n_blocks, length, LANES), F32)

    def tiles(*leading):
        return pltpu.VMEM(leading + (SUB, LANES), F32)

    signal = jax.ShapeDtypeStruct((length, channels), jnp.bfloat16)
    hbm = pl.BlockSpec(memory_space=pltpu.HBM)
    vmem = pl.BlockSpec(memory_space=pltpu.VMEM)
    n_parts = n_blocks // piece_blocks
    wide_rows = [pltpu.VMEM((length, channels), jnp.bfloat16) for _ in range(4)]
    results = pl.pallas_call(
        functools.partial(kernel, n_ctx, n_seq, n_parts),
        out_shape=[signal] * 4 + [jax.ShapeDtypeStruct((n_tiles, SUB, LANES), F32)],
        in_specs=[hbm] * 4 + [vmem],
        out_specs=[vmem] * 5,
        scratch_shapes=wide_rows
        + [rows() for _ in range(8)]
        + [tiles(n_tiles, SUB), tiles(n_tiles, SUB)]
        + [tiles(piece_blocks, halves, SUB) for _ in range(2)]
        + [pltpu.VMEM((piece_blocks, length, LANES), F32) for _ in range(4)]
        + [pltpu.VMEM((n_blocks, modes, LANES), F32) for _ in range(3)]
        + [tiles(n_tiles), tiles(n_tiles)]
        + [
            tiles(n_tiles, 2), tiles(LOCAL, per_owner, 2), tiles(LOCAL, per_owner, 2), tiles(n_tiles, 2),
            tiles(per_owner), tiles(per_owner), tiles(n_groups, per_owner),
            tiles(per_owner), tiles(n_groups * n_seq, per_sum), tiles(n_tiles), tiles(n_ctx, per_sum), tiles(per_sum),
        ]
        + [pltpu.SemaphoreType.DMA((LOCAL, owner_pieces)) for _ in range(4)]
        + [pltpu.SemaphoreType.DMA((n_groups,)) for _ in range(2)]
        + [pltpu.SemaphoreType.DMA((n_groups * n_seq,)) for _ in range(2)]
        + [pltpu.SemaphoreType.DMA((n_ctx,)) for _ in range(4)]
        + [pltpu.SemaphoreType.DMA((4, n_parts)), pltpu.SemaphoreType.DMA],
        compiler_params=pltpu.CompilerParams(
            collective_id=0, has_side_effects=True, vmem_limit_bytes=820 * 64 * 1024
        ),
        cost_estimate=pl.CostEstimate(flops=100_000_000, bytes_accessed=4_500_000, transcendentals=1_000_000),
        name="modal_states",
    )(query_input[0], key_input[0], value_input[0], cotangent[0], jnp.concatenate([decay_rates.T, residues.T], axis=0))
    results = pl.pallas_call(
        writer,
        out_shape=[signal] * 4 + [jax.ShapeDtypeStruct((modes, channels), F32)],
        in_specs=[vmem] * 5,
        out_specs=[hbm] * 5,
        scratch_shapes=[
            pltpu.VMEM((4 * length, channels), jnp.bfloat16), pltpu.VMEM((modes, channels), F32),
            pltpu.SemaphoreType.DMA((4, 4)), pltpu.SemaphoreType.DMA,
        ],
        compiler_params=pltpu.CompilerParams(vmem_limit_bytes=16 * 1024 * 1024),
        cost_estimate=pl.CostEstimate(flops=300_000_000, bytes_accessed=4_500_000, transcendentals=0),
        name="token_order",
    )(*results)
    return tuple(array[None] for array in results[:4]) + (results[4].T,)


def solution(mesh):
    wide = P("seq", "ctx", None)
    return jax.shard_map(
        functools.partial(on_device, mesh.shape["ctx"], mesh.shape["seq"]),
        mesh=mesh,
        in_specs=(wide, wide, wide, wide, P(), P()),
        out_specs=(wide, wide, wide, wide, P()),
        check_vma=False,
    )
```

```python
import functools

import jax
import jax.numpy as jnp
from jax import lax
from jax.experimental import pallas as pl
from jax.experimental.pallas import tpu as pltpu
from jax.sharding import PartitionSpec as P

SUB = 8
LANES = 128
LOCAL = 4
MESH = pl.DeviceIdType.MESH
F32 = jnp.float32


def one_minus_exp(u):
    total = jnp.ones_like(u)
    for order in range(8, 1, -1):
        total = 1.0 - (u / order) * total
    return u * total


def columns_of(block):
    return pl.ds(pl.multiple_of(block * LANES, LANES), LANES)


def step_order(length, steps, inverse):
    row = lax.broadcasted_iota(jnp.int32, (length, length), 0)
    col = lax.broadcasted_iota(jnp.int32, (length, length), 1)
    if inverse:
        row, col = col, row
    return jnp.where(col == steps * (row % SUB) + row // SUB, 1.0, 0.0).astype(jnp.bfloat16)


def kernel(
    n_ctx, n_seq, n_parts, query_hbm, key_hbm, value_hbm, cot_hbm, param_ref,
    out, grad_query, grad_key, grad_value, grad_all,
    query, key, value, cot,
    query_p, key_p, value_p, cot_p, mix_p, adj_p, conv_p, back_p, before, after, up_turn, down_turn,
    lam_row, lam16_row, weight_row, rate_tile, scale_tile,
    state_out, state_in, carry_out, carry_in, hop_up, hop_down, hop_in,
    cross_out, cross_in, lag_out, lag_in, grad_own,
    state_send, state_recv, carry_send, carry_recv, hop_send, hop_recv, cross_send, cross_recv,
    lag_send, lag_recv, grad_send, grad_recv, load_sem, own_sem,
):
    me = lax.axis_index("ctx")
    my_seq = lax.axis_index("seq")
    length, channels = query.shape
    modes = param_ref.shape[0] // 2
    steps = length // SUB
    n_blocks = channels // LANES
    halves = modes // SUB
    n_tiles = n_blocks * halves
    n_groups = n_ctx // LOCAL
    my_group, my_local = me // LOCAL, lax.rem(me, LOCAL)
    per_owner = n_tiles // LOCAL
    per_sum = per_owner // n_groups
    owner_blocks = per_owner // halves
    piece_blocks = max(1, owner_blocks // 2)
    owner_pieces = owner_blocks // piece_blocks
    piece_tiles = piece_blocks * halves
    n_pieces = n_blocks // piece_blocks
    part = channels // n_parts

    def load(index, place):
        cols = pl.ds(pl.multiple_of(place * part, LANES), part)
        source = (key_hbm, value_hbm, query_hbm, cot_hbm)[index]
        target = (key, value, query, cot)[index]
        return pltpu.make_async_copy(source.at[:, cols], target.at[:, cols], load_sem.at[index, place])

    for place in range(n_parts):
        for index in range(4):
            load(index, place).start()

    def peer(distance):
        return lax.rem(me + distance, n_ctx)

    def seq_peer(distance):
        return lax.rem(my_seq + distance, n_seq)

    def remote(src, dst, send, recv, target):
        return pltpu.make_async_remote_copy(
            src_ref=src, dst_ref=dst, send_sem=send, recv_sem=recv,
            device_id=target, device_id_type=MESH,
        )

    def piece_of(ref, piece):
        return ref.at[pl.ds(piece * piece_tiles, piece_tiles)]

    def sum_start(owner):
        return lax.rem(owner, LOCAL) * per_owner + owner // LOCAL * per_sum

    def summed(ref, owner):
        return ref.at[pl.ds(sum_start(owner), per_sum)]

    def state_copy(owner, place, slot):
        return remote(
            piece_of(state_out, owner * owner_pieces + place), piece_of(state_in.at[slot], place),
            state_send.at[owner, place], state_recv.at[slot, place], {"ctx": my_group * LOCAL + owner},
        )

    def carry_copy(target, place, slot):
        return remote(
            piece_of(carry_out.at[target], place), piece_of(carry_in, slot * owner_pieces + place),
            carry_send.at[target, place], carry_recv.at[slot, place], {"ctx": my_group * LOCAL + target},
        )

    def hop_copy(source, target, slot):
        return remote(source, hop_in.at[slot], hop_send.at[target], hop_recv.at[slot], {"ctx": target * LOCAL + my_local})

    def cross_copy(target, target_seq, slot):
        return remote(
            cross_out.at[pl.ds(target * per_sum, per_sum)], cross_in.at[slot],
            cross_send.at[target * n_seq + target_seq], cross_recv.at[slot],
            {"ctx": target * LOCAL + my_local, "seq": target_seq},
        )

    def lag_copy(owner, slot):
        return remote(summed(lag_out, owner), lag_in.at[slot], lag_send.at[owner], lag_recv.at[slot], {"ctx": owner})

    def grad_copy(target, slot):
        return remote(grad_own, summed(grad_all, slot), grad_send.at[target], grad_recv.at[slot], {"ctx": target})

    barrier = pltpu.get_barrier_semaphore()
    for distance in range(1, n_ctx):
        pl.semaphore_signal(barrier, inc=1, device_id={"ctx": peer(distance)}, device_id_type=MESH)
    for distance in range(1, n_seq):
        for group in range(n_groups):
            target = {"ctx": lax.rem(my_group + group, n_groups) * LOCAL + my_local, "seq": seq_peer(distance)}
            pl.semaphore_signal(barrier, inc=1, device_id=target, device_id_type=MESH)

    for block in range(n_blocks):
        cols = slice(block * LANES, (block + 1) * LANES)
        rate = param_ref[:modes, cols]
        scale = jnp.sqrt(one_minus_exp(2.0 * rate))
        lam_row[block] = jnp.exp(-rate)
        lam16_row[block] = jnp.exp(-float(steps) * rate)
        weight_row[block] = param_ref[modes:, cols] * scale
        for half in range(halves):
            rows = slice(half * SUB, (half + 1) * SUB)
            rate_tile[block * halves + half] = rate[rows]
            scale_tile[block * halves + half] = scale[rows]

    to_steps = step_order(length, steps, False)

    def turn(place, _):
        cols = pl.ds(pl.multiple_of(place * part, LANES), part)
        for index in range(4):
            load(index, place).wait()
        key_here, value_here, query_here, cot_here = [
            jnp.dot(to_steps, ref[:, cols], preferred_element_type=F32) for ref in (key, value, query, cot)
        ]
        mixed = key_here * value_here
        adjoint = cot_here * query_here
        for inner in range(part // LANES):
            block = place * (part // LANES) + inner
            lanes = slice(inner * LANES, (inner + 1) * LANES)
            query_p[block] = query_here[:, lanes]
            key_p[block] = key_here[:, lanes]
            value_p[block] = value_here[:, lanes]
            cot_p[block] = cot_here[:, lanes]
            mix_p[block] = mixed[:, lanes]
            adj_p[block] = adjoint[:, lanes]
        return 0

    lax.fori_loop(0, n_parts, turn, 0)

    def wide(ref, block, mode):
        return jnp.broadcast_to(ref[block, pl.ds(mode, 1), :], (SUB, LANES))

    def half_rows(ref, block, half):
        return ref[block, half * SUB:(half + 1) * SUB, :]

    def rows_at(ref, block, step):
        return ref[block, step * SUB:(step + 1) * SUB, :]

    def tree(terms):
        while len(terms) > 1:
            terms = [sum(terms[place:place + 2][1:], terms[place]) for place in range(0, len(terms), 2)]
        return terms[0]

    def cut(array):
        return [array[step * SUB:(step + 1) * SUB] for step in range(steps)]

    def states_of(block, inner):
        for half in range(halves):
            lams = [wide(lam_row, block, half * SUB + mode) for mode in range(SUB)]
            lasts = [rows_at(mix_p, block, 0)] * SUB
            firsts = [rows_at(adj_p, block, steps - 1)] * SUB
            for step in range(1, steps):
                mix, adj = rows_at(mix_p, block, step), rows_at(adj_p, block, steps - 1 - step)
                lasts = [have * lam + mix for have, lam in zip(lasts, lams)]
                firsts = [have * lam + adj for have, lam in zip(firsts, lams)]
            for mode in range(SUB):
                up_turn[inner, half, mode] = lasts[mode]
                down_turn[inner, half, mode] = firsts[mode]
        for half in range(halves):
            tile = block * halves + half
            lam16 = half_rows(lam16_row, block, half)
            lasts = [up_turn[inner, half, :, chunk, :] for chunk in range(SUB)]
            firsts = [down_turn[inner, half, :, chunk, :] for chunk in range(SUB)]
            state = lasts[0]
            lag = jnp.zeros_like(state)
            for chunk in range(1, SUB):
                before[tile, chunk] = state
                lag = lag + firsts[chunk] * state
                state = state * lam16 + lasts[chunk]
            state_out[tile, 0] = state
            lag_out[tile] = lag
            state = firsts[-1]
            for chunk in range(SUB - 2, -1, -1):
                after[tile, chunk] = state
                state = state * lam16 + firsts[chunk]
            state_out[tile, 1] = state

    def first_pass(index, _):
        piece = lax.rem(owner_pieces * (my_local + 1) + index, n_pieces)
        for inner in range(piece_blocks):
            states_of(piece * piece_blocks + inner, inner)

        @pl.when(index == 0)
        def _():
            pl.semaphore_wait(barrier, n_ctx - 1 + (n_seq - 1) * n_groups)

        owner, place = piece // owner_pieces, lax.rem(piece, owner_pieces)

        @pl.when(owner != my_local)
        def _():
            state_copy(owner, place, my_local).start()

        @pl.when(owner == my_local)
        def _():
            state_in[my_local, pl.ds(place * piece_tiles, piece_tiles)] = state_out[pl.ds(piece * piece_tiles, piece_tiles)]

        return 0

    lax.fori_loop(0, n_pieces, first_pass, 0)

    def lag_terms(block):
        mix = cut(mix_p[block])
        adj = cut(adj_p[block])
        lam = [lam_row[block, pl.ds(half * SUB, SUB), :] for half in range(halves)]
        totals = [rows * mix[0] for rows in adj]
        for step in range(1, steps):
            for lag in range(steps - step):
                totals[lag] = totals[lag] + adj[step + lag] * mix[step]
        levels = [jnp.broadcast_to(jnp.sum(total, axis=0, keepdims=True), (SUB, LANES)) for total in totals]
        sums = [levels[-1]] * halves
        for level in levels[-2::-1]:
            sums = [have * left + level for have, left in zip(sums, lam)]
        for half in range(halves):
            tile = block * halves + half
            lag_out[tile] = sums[half] + lam[half] * lag_out[tile]

    def chunk_terms(block):
        mix = cut(mix_p[block])
        adj = cut(adj_p[block])
        lam = [lam_row[block, pl.ds(half * SUB, SUB), :] for half in range(halves)]
        power = [weight_row[block, pl.ds(half * SUB, SUB), :] for half in range(halves)]
        taps = []
        for step in range(steps):
            taps.append(jnp.broadcast_to(jnp.sum(sum(power), axis=0, keepdims=True), (SUB, LANES)))
            power = [left * right for left, right in zip(power, lam)]
        totals = [taps[0] * rows for rows in mix]
        for lag in range(1, steps):
            for step in range(lag, steps):
                totals[step] = totals[step] + taps[lag] * mix[step - lag]
        for step in range(steps):
            conv_p[block, step * SUB:(step + 1) * SUB, :] = totals[step]
        totals = [taps[0] * rows for rows in adj]
        for lag in range(1, steps):
            for step in range(steps - lag):
                totals[step] = totals[step] + taps[lag] * adj[step + lag]
        for step in range(steps):
            back_p[block, step * SUB:(step + 1) * SUB, :] = totals[step]
    def lag_pass(index, _):
        piece = lax.rem(owner_pieces * (my_local + 1) + index, n_pieces)
        for inner in range(piece_blocks):
            lag_terms(piece * piece_blocks + inner)
        for inner in range(piece_tiles // per_sum):
            start = piece * piece_tiles + inner * per_sum
            owner = lax.rem(start, per_owner) // per_sum * LOCAL + start // per_owner

            @pl.when(owner != me)
            def _():
                lag_copy(owner, me).start()

            @pl.when(owner == me)
            def _():
                lag_in[me] = lag_out[pl.ds(sum_start(me), per_sum)]

        return 0

    lax.fori_loop(0, n_pieces, lag_pass, 0)

    def second_pass(piece, _):
        for inner in range(piece_blocks):
            chunk_terms(piece * piece_blocks + inner)
        return 0

    def local_peer(distance):
        return lax.rem(my_local + distance, LOCAL)

    def group_peer(distance):
        return lax.rem(my_group + distance, n_groups)

    for distance in range(1, LOCAL):
        source = local_peer(LOCAL - distance)
        for place in range(owner_pieces):
            state_copy(source, place, source).wait_recv()
    my_first = my_local * per_owner
    for place in range(per_owner):
        hop = jnp.exp(-float(length) * rate_tile[my_first + place])
        carried = state_in[0, place, 0]
        for source in range(1, LOCAL):
            carry_out[source, place, 0] = carried
            carried = carried * hop + state_in[source, place, 0]
        hop_up[place] = carried
        carried = state_in[LOCAL - 1, place, 1]
        for source in range(LOCAL - 2, -1, -1):
            carry_out[source, place, 1] = carried
            carried = carried * hop + state_in[source, place, 1]
        hop_down[place] = carried
    for distance in range(1, n_groups):
        target = group_peer(distance)

        @pl.when(target > my_group)
        def _():
            hop_copy(hop_up, target, my_group).start()

        @pl.when(target < my_group)
        def _():
            hop_copy(hop_down, target, my_group).start()

    hop_in[my_group] = jnp.zeros((per_owner, SUB, LANES), F32)

    lax.fori_loop(0, 5 * n_pieces // 8, second_pass, 0)

    for distance in range(1, n_groups):
        source = group_peer(n_groups - distance)
        hop_copy(hop_up, source, source).wait_recv()
    for place in range(per_owner):
        rate = rate_tile[my_first + place]
        hop = jnp.exp(-float(length) * rate)
        far = jnp.exp(-float(length * LOCAL) * rate)
        carried = jnp.zeros((SUB, LANES), F32)
        for group in range(n_groups):
            carried = jnp.where(group < my_group, carried * far + hop_in[group, place], carried)
        cross = jnp.zeros((SUB, LANES), F32)
        for source in range(LOCAL):
            total = carry_out[source, place, 0] + carried if source else carried
            carry_out[source, place, 0] = total
            cross = cross + total * state_in[source, place, 1]
            carried = carried * hop
        cross_out[place] = jnp.exp(-rate) * cross
        carried = jnp.zeros((SUB, LANES), F32)
        for group in range(n_groups - 1, -1, -1):
            carried = jnp.where(group > my_group, carried * far + hop_in[group, place], carried)
        for source in range(LOCAL - 1, -1, -1):
            carry_out[source, place, 1] = carry_out[source, place, 1] + carried if source < LOCAL - 1 else carried
            carried = carried * hop
    for place in range(owner_pieces):
        for distance in range(1, LOCAL):
            carry_copy(local_peer(distance), place, my_local).start()
    carry_in[pl.ds(my_first, per_owner)] = carry_out[my_local]

    for distance in range(1, n_ctx):
        source = peer(n_ctx - distance)
        lag_copy(source, source).wait_recv()
    for place in range(per_sum):
        total = cross_out[my_group * per_sum + place]
        for source in range(n_ctx):
            total = total + lag_in[source, place]
        cross_out[my_group * per_sum + place] = total
    counterparts = [(group, seq) for group in range(n_groups) for seq in range(n_seq)][1:]
    my_slot = my_group * n_seq + my_seq
    for group, seq in counterparts:
        cross_copy(group_peer(group), seq_peer(seq), my_slot).start()
    cross_in[my_slot] = cross_out[pl.ds(my_group * per_sum, per_sum)]

    lax.fori_loop(5 * n_pieces // 8, n_pieces, second_pass, 0)

    def finish(block, inner):
        cols = columns_of(block)
        for half in range(halves):
            tile = block * halves + half
            lam16 = half_rows(lam16_row, block, half)
            lead = half_rows(lam_row, block, half) * half_rows(weight_row, block, half)
            state = carry_in[tile, 0]
            for chunk in range(SUB):
                up_turn[inner, half, chunk] = lead * (state + before[tile, chunk] if chunk else state)
                state = state * lam16
            state = carry_in[tile, 1]
            for chunk in range(SUB - 1, -1, -1):
                down_turn[inner, half, chunk] = lead * (state + after[tile, chunk] if chunk < SUB - 1 else state)
                state = state * lam16
        lams = [wide(lam_row, block, mode) for mode in range(modes)]

        def put(place, step, factor, pair):
            rows = pl.ds(step * SUB, 2 * SUB)
            target = (out, grad_query, grad_key, grad_value)[place]
            target[rows, cols] = (factor[block, rows, :] * pair).astype(jnp.bfloat16)

        terms = [up_turn[inner, mode // SUB, :, mode % SUB, :] for mode in range(modes)]
        sums = []
        for step in range(steps):
            sums.append(rows_at(conv_p, block, step) + tree(terms))
            terms = [term * lam for term, lam in zip(terms, lams)]
            if step % 2:
                pair = jnp.concatenate(sums, axis=0)
                put(0, step - 1, query_p, pair)
                put(1, step - 1, cot_p, pair)
                sums = []
        terms = [down_turn[inner, mode // SUB, :, mode % SUB, :] for mode in range(modes)]
        for step in range(steps - 1, -1, -1):
            sums.insert(0, rows_at(back_p, block, step) + tree(terms))
            terms = [term * lam for term, lam in zip(terms, lams)]
            if step % 2 == 0:
                pair = jnp.concatenate(sums, axis=0)
                put(2, step, value_p, pair)
                put(3, step, key_p, pair)
                sums = []

    own_copy = pltpu.make_async_copy(grad_own, summed(grad_all, me), own_sem)

    def last_pass(index, _):
        owner = lax.rem(my_local + LOCAL - index // owner_pieces, LOCAL)
        place = lax.rem(index, owner_pieces)

        @pl.when(owner != my_local)
        def _():
            carry_copy(owner, place, owner).wait_recv()

        for inner in range(piece_blocks):
            finish((owner * owner_pieces + place) * piece_blocks + inner, inner)

        @pl.when(index == n_pieces // 8)
        def _():
            for group, seq in counterparts:
                source, source_seq = group_peer(n_groups - group), seq_peer(n_seq - seq)
                cross_copy(source, source_seq, source * n_seq + source_seq).wait_recv()
            for place in range(per_sum):
                total = cross_in[0, place]
                for source in range(1, n_groups * n_seq):
                    total = total + cross_in[source, place]
                grad_own[place] = total * scale_tile[sum_start(me) + place] * (1.0 / (length * n_ctx * n_seq))
            for distance in range(1, n_ctx):
                grad_copy(peer(distance), me).start()
            own_copy.start()

        return 0

    lax.fori_loop(0, n_pieces, last_pass, 0)

    for distance in range(1, n_ctx):
        source = peer(n_ctx - distance)
        grad_copy(source, source).wait_recv()
    own_copy.wait()
    for distance in range(1, n_ctx):
        target = peer(distance)
        lag_copy(target, me).wait_send()
        grad_copy(target, me).wait_send()
    for distance in range(1, LOCAL):
        target = local_peer(distance)
        for place in range(owner_pieces):
            state_copy(target, place, my_local).wait_send()
            carry_copy(target, place, my_local).wait_send()
    for distance in range(1, n_groups):
        target = group_peer(distance)
        hop_copy(hop_up, target, my_group).wait_send()
    for group, seq in counterparts:
        cross_copy(group_peer(group), seq_peer(seq), my_slot).wait_send()


def writer(
    out_p, grad_query_p, grad_key_p, grad_value_p, grad_tiles, out, grad_query, grad_key, grad_value, grad_res,
    turned, grad_rows, store_sem, grad_sem,
):
    length, channels = out.shape
    n_parts = store_sem.shape[1]
    part = channels // n_parts
    halves = grad_res.shape[0] // SUB
    sources = (out_p, grad_query_p, grad_key_p, grad_value_p)
    targets = (out, grad_query, grad_key, grad_value)
    for tile in range(grad_tiles.shape[0]):
        block, half = divmod(tile, halves)
        grad_rows[half * SUB:(half + 1) * SUB, block * LANES:(block + 1) * LANES] = grad_tiles[tile]
    stores = [pltpu.make_async_copy(grad_rows, grad_res, grad_sem)]
    stores[-1].start()
    to_tokens = step_order(length, length // SUB, True)
    for place in range(n_parts):
        cols = slice(place * part, (place + 1) * part)
        for index in range(4):
            where = (slice(index * length, (index + 1) * length), cols)
            turned[where] = jnp.dot(to_tokens, sources[index][:, cols], preferred_element_type=F32).astype(jnp.bfloat16)
            stores.append(pltpu.make_async_copy(turned.at[where], targets[index].at[:, cols], store_sem.at[index, place]))
            stores[-1].start()
    for copy in stores:
        copy.wait()


def on_device(n_ctx, n_seq, query_input, key_input, value_input, cotangent, residues, decay_rates):
    _, length, channels = query_input.shape
    modes = residues.shape[1]
    n_blocks = channels // LANES
    halves = modes // SUB
    n_tiles = n_blocks * halves
    n_groups = n_ctx // LOCAL
    per_owner = n_tiles // LOCAL
    per_sum = per_owner // n_groups
    piece_blocks = max(1, per_owner // halves // 2)
    owner_pieces = per_owner // halves // piece_blocks

    def rows():
        return pltpu.VMEM((n_blocks, length, LANES), F32)

    def tiles(*leading):
        return pltpu.VMEM(leading + (SUB, LANES), F32)

    signal = jax.ShapeDtypeStruct((length, channels), jnp.bfloat16)
    hbm = pl.BlockSpec(memory_space=pltpu.HBM)
    vmem = pl.BlockSpec(memory_space=pltpu.VMEM)
    n_parts = 4
    wide_rows = [pltpu.VMEM((length, channels), jnp.bfloat16) for _ in range(4)]
    results = pl.pallas_call(
        functools.partial(kernel, n_ctx, n_seq, n_parts),
        out_shape=[signal] * 4 + [jax.ShapeDtypeStruct((n_tiles, SUB, LANES), F32)],
        in_specs=[hbm] * 4 + [vmem],
        out_specs=[vmem] * 5,
        scratch_shapes=wide_rows
        + [rows() for _ in range(8)]
        + [tiles(n_tiles, SUB), tiles(n_tiles, SUB)]
        + [tiles(piece_blocks, halves, SUB) for _ in range(2)]
        + [pltpu.VMEM((n_blocks, modes, LANES), F32) for _ in range(3)]
        + [tiles(n_tiles), tiles(n_tiles)]
        + [
            tiles(n_tiles, 2), tiles(LOCAL, per_owner, 2), tiles(LOCAL, per_owner, 2), tiles(n_tiles, 2),
            tiles(per_owner), tiles(per_owner), tiles(n_groups, per_owner),
            tiles(per_owner), tiles(n_groups * n_seq, per_sum), tiles(n_tiles), tiles(n_ctx, per_sum), tiles(per_sum),
        ]
        + [pltpu.SemaphoreType.DMA((LOCAL, owner_pieces)) for _ in range(4)]
        + [pltpu.SemaphoreType.DMA((n_groups,)) for _ in range(2)]
        + [pltpu.SemaphoreType.DMA((n_groups * n_seq,)) for _ in range(2)]
        + [pltpu.SemaphoreType.DMA((n_ctx,)) for _ in range(4)]
        + [pltpu.SemaphoreType.DMA((4, n_parts)), pltpu.SemaphoreType.DMA],
        compiler_params=pltpu.CompilerParams(
            collective_id=0, has_side_effects=True, vmem_limit_bytes=820 * 64 * 1024
        ),
        cost_estimate=pl.CostEstimate(flops=100_000_000, bytes_accessed=4_500_000, transcendentals=1_000_000),
        name="modal_states",
    )(query_input[0], key_input[0], value_input[0], cotangent[0], jnp.concatenate([decay_rates.T, residues.T], axis=0))
    results = pl.pallas_call(
        writer,
        out_shape=[signal] * 4 + [jax.ShapeDtypeStruct((modes, channels), F32)],
        in_specs=[vmem] * 5,
        out_specs=[hbm] * 5,
        scratch_shapes=[
            pltpu.VMEM((4 * length, channels), jnp.bfloat16), pltpu.VMEM((modes, channels), F32),
            pltpu.SemaphoreType.DMA((4, n_parts)), pltpu.SemaphoreType.DMA,
        ],
        compiler_params=pltpu.CompilerParams(vmem_limit_bytes=16 * 1024 * 1024),
        cost_estimate=pl.CostEstimate(flops=300_000_000, bytes_accessed=4_500_000, transcendentals=0),
        name="token_order",
    )(*results)
    return tuple(array[None] for array in results[:4]) + (results[4].T,)


def solution(mesh):
    wide = P("seq", "ctx", None)
    return jax.shard_map(
        functools.partial(on_device, mesh.shape["ctx"], mesh.shape["seq"]),
        mesh=mesh,
        in_specs=(wide, wide, wide, wide, P(), P()),
        out_specs=(wide, wide, wide, wide, P()),
        check_vma=False,
    )
```
